128 devices in a mesh: rx: 8 (over z, core), ry: 16 (over x, y).
Axes of the slice: x: 4, y: 4, z: 4, core: 2. Of those that a mesh axis runs over, the one named last changes fastest.
Arguments:
- features: bfloat16 [1024, 64, 512], P(('rx', 'ry')), may hold values from -6 to 6
- grad_out: bfloat16 [1024, 64, 512], P(('rx', 'ry')), may hold values from -6 to 6
- weights: bfloat16 [27, 64, 64], replicated, may hold values from -0.15625 to 0.15625
- live_count: int32 [128], P(('rx', 'ry')), may hold values from 0 to 8, as said below
- neighbor: int32 [1024, 6], P(('rx', 'ry')), may hold values from -1 to 23, as said below
- send_list: int32 [512, 4], P(('rx', 'ry')), may hold values from -1 to 7, as said below
Outputs:
- output: bfloat16 [1024, 64, 512], P(('rx', 'ry'))
- grad_features: bfloat16 [1024, 64, 512], P(('rx', 'ry'))
- grad_weights: float32 [27, 64, 64], replicated
The draws below stay inside these ranges and needn't reach their ends.
Inputs may be any that keep to these rules, and one draw needn't show every extreme that they name: A device's occupied bricks take its first live_count slots; some device is full. `neighbor`: only live slots have entries other than -1. Entries of 8 or more stand only in columns 0 to 3, equal 8 + s * 4 + k in column s, and never point beyond the grid of devices. Sides 4 and 5 are always within the device. Adjacency is mutual: a brick is its neighbour's neighbour on the opposite side, and each received face slot of a side is used by at most one brick. `send_list`: row 4 d + t lists distinct live slots of device d, their face t going to the device beside d on side t; used entries come first, then -1.
All inputs are finite; a program needn't handle non-finite values.
Results may differ from the reference program's by a relative error of at most 0.0025.
Values may be sent and summed in bfloat16 or wider, within the bound.
No kernel may reach another device: no remote copies, remote signals or barrier semaphores. Data moves between devices by JAX's collectives and lax.ppermute only.
A program may use at most 64 MiB of HBM per device.

```python
import jax
import jax.numpy as jnp
from jax import lax

C = 64
RB = 2
H = 2
B_DEV = 8
CAP = 4
BRICKS = 1024
N_RX = 8
N_RY = 16


def shift_low(values, axis):
    first = jnp.zeros_like(lax_take(values, axis, 0, 1))
    rest = lax_take(values, axis, 0, values.shape[axis] - 1)
    return jnp.concatenate([first, rest], axis=axis)


def shift_high(values, axis):
    last = jnp.zeros_like(lax_take(values, axis, 0, 1))
    rest = lax_take(values, axis, 1, values.shape[axis] - 1)
    return jnp.concatenate([rest, last], axis=axis)


def lax_take(values, axis, start, length):
    return jnp.take(values, jnp.arange(start, start + length), axis=axis)


def local_value(occupied, slot_rank):
    return jnp.where(occupied == 1, slot_rank, -1)


def pair_keys(pairs):
    shape = pairs.shape
    flat_pairs = pairs.reshape(shape[0], shape[1], -1)
    return (jnp.cumsum(flat_pairs, axis=-1) - 1).reshape(shape).astype(jnp.int32)


def build_bricks(key):
    subkeys = jax.random.split(jax.random.fold_in(key, 4242), 4)
    positions = RB * RB * H
    devices = N_RX * N_RY
    fill_rate = jax.random.randint(subkeys[0], (N_RX, N_RY), 40, 101)
    full_row = jax.random.randint(subkeys[1], (), 0, N_RX - 1)
    full_col = jax.random.randint(subkeys[2], (), 0, N_RY - 1)
    grid_rows = jnp.arange(N_RX)[:, None]
    grid_cols = jnp.arange(N_RY)[None, :]
    full = (grid_rows == full_row) & (grid_cols == full_col) | (grid_rows == full_row + 1) & (grid_cols == full_col) | (grid_rows == full_row) & (grid_cols == full_col + 1)
    fill_rate = jnp.where(full, 101, fill_rate)
    rolls = jax.random.randint(subkeys[3], (N_RX, N_RY, RB, RB, H), 0, 100)
    occupied = (rolls < fill_rate[:, :, None, None, None]).astype(jnp.int32)
    flat_occ = occupied.reshape(N_RX, N_RY, positions)
    slot_rank = (jnp.cumsum(flat_occ, axis=-1) - 1).reshape(occupied.shape).astype(jnp.int32)
    count = flat_occ.sum(-1).reshape(devices).astype(jnp.int32)
    pair_x = occupied[:-1, :, RB - 1] * occupied[1:, :, 0]
    key_x = pair_keys(pair_x)
    pad_x = jnp.zeros((1, N_RY, RB, H), jnp.int32)
    pair_x_low = jnp.concatenate([pad_x, pair_x], 0)
    key_x_low = jnp.concatenate([pad_x, key_x], 0)
    pair_x_high = jnp.concatenate([pair_x, pad_x], 0)
    key_x_high = jnp.concatenate([key_x, pad_x], 0)
    pair_y = occupied[:, :-1, :, RB - 1] * occupied[:, 1:, :, 0]
    key_y = pair_keys(pair_y)
    pad_y = jnp.zeros((N_RX, 1, RB, H), jnp.int32)
    pair_y_low = jnp.concatenate([pad_y, pair_y], 1)
    key_y_low = jnp.concatenate([pad_y, key_y], 1)
    pair_y_high = jnp.concatenate([pair_y, pad_y], 1)
    key_y_high = jnp.concatenate([key_y, pad_y], 1)
    index_x = jnp.arange(RB)[:, None, None]
    index_y = jnp.arange(RB)[None, :, None]
    side_zero = jnp.where(index_x > 0, local_value(shift_low(occupied, 2), shift_low(slot_rank, 2)), jnp.where(pair_x_low[:, :, None] == 1, positions + key_x_low[:, :, None], -1))
    side_one = jnp.where(index_x < RB - 1, local_value(shift_high(occupied, 2), shift_high(slot_rank, 2)), jnp.where(pair_x_high[:, :, None] == 1, positions + CAP + key_x_high[:, :, None], -1))
    side_two = jnp.where(index_y > 0, local_value(shift_low(occupied, 3), shift_low(slot_rank, 3)), jnp.where(pair_y_low[:, :, :, None] == 1, positions + 2 * CAP + key_y_low[:, :, :, None], -1))
    side_three = jnp.where(index_y < RB - 1, local_value(shift_high(occupied, 3), shift_high(slot_rank, 3)), jnp.where(pair_y_high[:, :, :, None] == 1, positions + 3 * CAP + key_y_high[:, :, :, None], -1))
    side_four = local_value(shift_low(occupied, 4), shift_low(slot_rank, 4))
    side_five = local_value(shift_high(occupied, 4), shift_high(slot_rank, 4))
    sides = jnp.stack([side_zero, side_one, side_two, side_three, side_four, side_five], axis=-1)
    sides = jnp.where(occupied[..., None] == 1, sides, -1).astype(jnp.int32)
    slot_of = jnp.where(occupied == 1, slot_rank, positions).reshape(devices, positions)
    device_ids = jnp.broadcast_to(jnp.arange(devices)[:, None], (devices, positions))
    table = jnp.full((devices, positions + 1, 6), -1, jnp.int32)
    table = table.at[device_ids, slot_of].set(sides.reshape(devices, positions, 6))
    neighbor = table[:, :positions].reshape(devices * positions, 6)

    def sender(pairs, keys, slots):
        target = jnp.where(pairs == 1, keys, CAP).reshape(devices, -1)
        owners = jnp.broadcast_to(jnp.arange(devices)[:, None], target.shape)
        listed = jnp.full((devices, CAP + 1), -1, jnp.int32)
        listed = listed.at[owners, target].set(slots.reshape(devices, -1).astype(jnp.int32))
        return listed[:, :CAP]
    send_zero = sender(pair_x_low, key_x_low, slot_rank[:, :, 0])
    send_one = sender(pair_x_high, key_x_high, slot_rank[:, :, RB - 1])
    send_two = sender(pair_y_low, key_y_low, slot_rank[:, :, :, 0])
    send_three = sender(pair_y_high, key_y_high, slot_rank[:, :, :, RB - 1])
    send_list = jnp.stack([send_zero, send_one, send_two, send_three], axis=1).reshape(devices * 4, CAP)
    return (count, neighbor, send_list)


def draw_live_count(key, part):
    return build_bricks(key)[0]


def draw_neighbor(key, part):
    return build_bricks(key)[1]


def draw_send_list(key, part):
    return build_bricks(key)[2]


def level_of(stream_key, dims, cuts, smallest, high):
    def one(position, shards_of):
        steps = jax.random.uniform(jax.random.fold_in(jax.random.fold_in(stream_key, 6), position), (shards_of,), jnp.float32, smallest / len(cuts), high / len(cuts))
        return jnp.repeat(jnp.exp(steps), dims[position] // shards_of).reshape((-1,) + (1,) * (len(dims) - position - 1))

    level = one(*cuts[0])
    for cut in cuts[1:]:
        level = level * one(*cut)
    return level


def gaussian(rng, shape, width, limit, shards=(), held_as=jnp.bfloat16):
    level = level_of(rng, shape, shards, -0.22, 0.18) if shards else 1.0
    values = jax.random.normal(rng, shape, jnp.float32) * width * level
    return jnp.minimum(jnp.maximum(values, -limit), limit).astype(held_as)


def setup_inputs(seed: int = 0) -> dict:
    arg_keys = jax.random.split(jax.random.key(seed), 7)
    return {
        "features": gaussian(arg_keys[0], (BRICKS, C, 512), 1.0, 6.0, ((0, 128),)),
        "grad_out": gaussian(arg_keys[1], (BRICKS, C, 512), 1.0, 6.0, ((0, 128),)),
        "weights": gaussian(arg_keys[2], (27, C, C), (27 * C) ** -0.5, 0.15625),
        "live_count": draw_live_count(jax.random.fold_in(arg_keys[6], 71), 0),
        "neighbor": draw_neighbor(jax.random.fold_in(arg_keys[6], 71), 0),
        "send_list": draw_send_list(jax.random.fold_in(arg_keys[6], 71), 0),
    }


def face_of(cube, s):
    n, c = (cube.shape[0], cube.shape[1])
    if s == 0:
        layer = cube[:, :, 0]
    elif s == 1:
        layer = cube[:, :, 7]
    elif s == 2:
        layer = cube[:, :, :, 0]
    elif s == 3:
        layer = cube[:, :, :, 7]
    elif s == 4:
        layer = cube[:, :, :, :, 0]
    else:
        layer = cube[:, :, :, :, 7]
    return layer.reshape(n, c, 64)

def halo_index(s):
    every = slice(None)
    within = slice(1, 9)
    table = [(every, every, 0, within, within), (every, every, 9, within, within), (every, every, within, 0, within), (every, every, within, 9, within), (every, every, within, within, 0), (every, every, within, within, 9)]
    return table[s]

def face_index(s):
    every = slice(None)
    table = [(every, every, 0), (every, every, 7), (every, every, every, 0), (every, every, every, 7), (every, every, every, every, 0), (every, every, every, every, 7)]
    return table[s]

def put_halo(bordered_volume, s, layer):
    n, c = (bordered_volume.shape[0], bordered_volume.shape[1])
    return bordered_volume.at[halo_index(s)].set(layer.reshape(n, c, 8, 8))

def take_halo(bordered_volume, s):
    n, c = (bordered_volume.shape[0], bordered_volume.shape[1])
    return bordered_volume[halo_index(s)].reshape(n, c, 64)

def add_face(cube, s, layer):
    n, c = (cube.shape[0], cube.shape[1])
    return cube.at[face_index(s)].add(layer.reshape(n, c, 8, 8))

def window_stack(bordered_volume):
    n, c = (bordered_volume.shape[0], bordered_volume.shape[1])
    shifted = []
    for a in range(3):
        for b in range(3):
            for d in range(3):
                shifted.append(bordered_volume[:, :, a:a + 8, b:b + 8, d:d + 8].reshape(n, c, 512))
    return jnp.concatenate(shifted, axis=1)

def convolve(bordered_volume, weight_matrix):
    return jnp.einsum('ah,thp->tap', weight_matrix, window_stack(bordered_volume), precision=lax.Precision.HIGHEST)

def reference(features, grad_out, weights, live_count, neighbor, send_list):
    devices = N_RX * N_RY
    total = features.shape[0]
    chans = features.shape[1]
    device = jnp.arange(total, dtype=jnp.int32) // B_DEV
    grid_row = device // N_RY
    grid_col = device % N_RY
    live_mask = jnp.arange(total, dtype=jnp.int32) % B_DEV < live_count[device]
    feat_live = jnp.where(live_mask[:, None, None], features, jnp.zeros_like(features))
    grad_live = jnp.where(live_mask[:, None, None], grad_out, jnp.zeros_like(grad_out))
    sources = []
    for s in range(6):
        entry_val = neighbor[:, s]
        source = jnp.where((entry_val >= 0) & (entry_val < B_DEV), device * B_DEV + entry_val, total)
        if s < 4:
            k = jnp.clip((entry_val - B_DEV) % CAP, 0, CAP - 1)
            peer_row = jnp.clip(grid_row + [-1, 1, 0, 0][s], 0, N_RX - 1)
            peer_col = jnp.clip(grid_col + [0, 0, -1, 1][s], 0, N_RY - 1)
            peer_dev = peer_row * N_RY + peer_col
            slot_index = send_list[peer_dev * 4 + (s ^ 1), k]
            remote = (entry_val >= B_DEV) & (slot_index >= 0)
            source = jnp.where(remote, peer_dev * B_DEV + slot_index, source)
        sources.append(source.astype(jnp.int32))
    source = jnp.stack(sources, axis=1)
    feat_cube = feat_live.reshape(total, chans, 8, 8, 8)
    faces = jnp.stack([face_of(feat_cube, s) for s in range(6)], axis=1)
    faces = jnp.concatenate([faces, jnp.zeros((1, 6, chans, 64), features.dtype)], axis=0)
    weight_matrix = weights.astype(jnp.float32).transpose(1, 0, 2).reshape(chans, 27 * chans)

    def one_device(inputs):
        feat_block, gradient_tile, block_src = inputs
        bordered_volume = jnp.pad(feat_block.reshape(B_DEV, chans, 8, 8, 8), ((0, 0), (0, 0), (1, 1), (1, 1), (1, 1)))
        for s in range(6):
            bordered_volume = put_halo(bordered_volume, s, faces[block_src[:, s], s ^ 1])
        output, pull_back = jax.vjp(convolve, bordered_volume.astype(jnp.float32), weight_matrix)
        grad_pad, grad_w = pull_back(gradient_tile.astype(jnp.float32))
        interior = grad_pad[:, :, 1:9, 1:9, 1:9].reshape(B_DEV, chans, 512)
        returned = jnp.stack([take_halo(grad_pad, s) for s in range(6)], axis=1)
        return (output.astype(jnp.bfloat16), interior, returned, grad_w)
    results = lax.map(one_device, (feat_live.reshape(devices, B_DEV, chans, 512), grad_live.reshape(devices, B_DEV, chans, 512), source.reshape(devices, B_DEV, 6)))
    output = results[0].reshape(total, chans, 512)
    interior = results[1].reshape(total, chans, 512)
    returned = results[2].reshape(total, 6, chans, 64)
    grad_w = lax.optimization_barrier(jnp.sum(results[3], axis=0))
    collected = jnp.zeros((total + 1, 6, chans, 64), jnp.float32)
    for s in range(6):
        collected = collected.at[source[:, s], s ^ 1].add(returned[:, s])
    grad_cube = interior.reshape(total, chans, 8, 8, 8)
    for s in range(6):
        grad_cube = add_face(grad_cube, s, collected[:total, s])
    output = jnp.where(live_mask[:, None, None], output, jnp.zeros_like(output))
    grad_features = jnp.where(live_mask[:, None, None], grad_cube.reshape(total, chans, 512), 0.0).astype(jnp.bfloat16)
    grad_weights = grad_w.reshape(chans, 27, chans).transpose(1, 0, 2) * (512.0 * total) ** (-0.5)
    return (output, grad_features, grad_weights)
```

```python
import jax
import jax.numpy as jnp
from jax import lax
from jax.experimental import pallas as pl
from jax.experimental.pallas import tpu as pltpu
from jax.sharding import Mesh
from jax.sharding import PartitionSpec as P

BF = jnp.bfloat16
F32 = jnp.float32
VMEM_SPEC = pl.BlockSpec(memory_space=pltpu.VMEM)
SMEM_SPEC = pl.BlockSpec(memory_space=pltpu.SMEM)
SLOTS = 8
CAP = 4
NONE = SLOTS + CAP
CELLS = 512
WIDE = 640


def lane(rows, cols):
    return lax.broadcasted_iota(jnp.int32, (rows, cols), 1)


def spin(x, amount):
    return pltpu.roll(x, amount % 128, 1)


def column(x, v):
    return x[:, 128 * v : 128 * v + 128]


def faces_kernel(send_ref, feat_ref, grad_ref, o0, o1, o2, o3):
    low = lane(64, 128) < 64
    zero = jnp.zeros((64, 128), BF)
    for k in range(CAP):
        e = send_ref[0, k]
        s = jnp.maximum(e, 0)
        v = jnp.where(low, feat_ref[s, :, 0:128], spin(grad_ref[s, :, 0:128], 64))
        o0[k] = jnp.where(e >= 0, v, zero)
        e = send_ref[1, k]
        s = jnp.maximum(e, 0)
        v = jnp.where(low, spin(feat_ref[s, :, 384:512], 64), grad_ref[s, :, 384:512])
        o1[k] = jnp.where(e >= 0, v, zero)
    cell = lax.broadcasted_iota(jnp.int32, (CELLS, 128), 0)
    spot = lane(CELLS, 128)
    same = (cell // 64 == spot // 8 % 8) & (cell % 8 == spot % 8)
    for t, j, o in ((2, 0, o2), (3, 7, o3)):
        on = same & (cell // 8 % 8 == j)
        pick_feat = jnp.where(on & (spot < 64), 1.0, 0.0).astype(BF)
        pick_grad = jnp.where(on & (spot >= 64), 1.0, 0.0).astype(BF)
        slot = [send_ref[t, k] for k in range(CAP)]
        feats = jnp.concatenate([feat_ref[jnp.maximum(e, 0)] for e in slot], 0)
        grads = jnp.concatenate([grad_ref[jnp.maximum(e, 0)] for e in slot], 0)
        both = jnp.dot(feats, pick_feat, preferred_element_type=F32) + jnp.dot(
            grads, pick_grad, preferred_element_type=F32
        )
        both = both.astype(BF)
        for k in range(CAP):
            o[k] = jnp.where(slot[k] >= 0, both[64 * k : 64 * k + 64], zero)


def fill_tables(live_ref, feat_ref, grad_ref, r0, r1, r2, r3, cubes, xface, yface):
    low = lane(64, 128) < 64
    row = lane(64, 128) // 8 % 8
    zero = jnp.zeros((64, 128), BF)
    for n, ref in enumerate((feat_ref, grad_ref)):
        for e in range(SLOTS):
            alive = e < live_ref[0]
            cols = [jnp.where(alive, ref[e, :, 128 * v : 128 * v + 128], zero) for v in range(4)]
            for v in range(4):
                cubes[n, e, :, 128 * v : 128 * v + 128] = cols[v]
                yface[n, 0, e, :, 128 * v : 128 * v + 128] = jnp.where(
                    row == 0, spin(cols[v], -56), zero
                )
                yface[n, 1, e, :, 128 * v : 128 * v + 128] = jnp.where(
                    row == 7, spin(cols[v], 56), zero
                )
            xface[n, 0, e] = jnp.where(low, zero, cols[3])
            xface[n, 1, e] = jnp.where(low, cols[0], zero)
        cubes[n, SLOTS] = jnp.zeros((64, CELLS), BF)
        for side in range(2):
            xface[n, side, NONE] = zero
            yface[n, side, NONE] = jnp.zeros((64, CELLS), BF)
    for k in range(CAP):
        a, b = r0[k], r1[k]
        xface[0, 0, SLOTS + k] = jnp.where(low, zero, spin(a, 64))
        xface[1, 0, SLOTS + k] = jnp.where(low, zero, a)
        xface[0, 1, SLOTS + k] = jnp.where(low, b, zero)
        xface[1, 1, SLOTS + k] = jnp.where(low, spin(b, 64), zero)
    spot = lax.broadcasted_iota(jnp.int32, (128, CELLS), 0)
    cell = lane(128, CELLS)
    same = (cell // 64 == spot // 8 % 8) & (cell % 8 == spot % 8)
    for side, j, r in ((0, 0, r2), (1, 7, r3)):
        packed = r[...].reshape(CAP * 64, 128)
        on = same & (cell // 8 % 8 == j)
        for n, part in enumerate((spot < 64, spot >= 64)):
            put = jnp.where(on & part, 1.0, 0.0).astype(BF)
            full = jnp.dot(packed, put, preferred_element_type=F32).astype(BF)
            for k in range(CAP):
                yface[n, side, SLOTS + k] = full[64 * k : 64 * k + 64]


def fill_windows(n, g, nb_ref, cubes, xface, yface, dst, base):
    def slot(side):
        e = nb_ref[g, side]
        near = jnp.minimum(e, SLOTS - 1)
        far = SLOTS + ((e - SLOTS) & (CAP - 1))
        return jnp.where(e < 0, NONE, jnp.where(e < SLOTS, near, far))

    def inner(side):
        e = nb_ref[g, side]
        return jnp.where(e < 0, SLOTS, jnp.minimum(e, SLOTS - 1))

    i0, i1, i2, i3 = (slot(s) for s in range(4))
    i4, i5 = inner(4), inner(5)
    spots = lane(64, 128)
    first_j, last_j = spots // 8 % 8 == 0, spots // 8 % 8 == 7
    first_k, last_k = spots % 8 == 0, spots % 8 == 7
    zero = jnp.zeros((64, 128), BF)
    for v in range(5):
        if v < 4:
            at = slice(128 * v, 128 * v + 128)
            mid = cubes[n, g, :, at]
            before = spin(cubes[n, i4, :, at], -7)
            after = spin(cubes[n, i5, :, at], 7)
            edge = yface[n, 0, i2, :, at] + yface[n, 1, i3, :, at]
            edges = (
                jnp.where(first_k, zero, spin(edge, 1)),
                edge,
                jnp.where(last_k, zero, spin(edge, -1)),
            )
        else:
            mid = xface[n, 0, i0] + xface[n, 1, i1]
            before, after = zero, zero
            edges = (zero, zero, zero)
        along = (
            jnp.where(first_k, before, spin(mid, 1)),
            mid,
            jnp.where(last_k, after, spin(mid, -1)),
        )
        to = pl.ds(base + 128 * v, 128)
        for c in range(3):
            dst[64 * c : 64 * c + 64, to] = jnp.where(first_j, edges[c], spin(along[c], 8))
            dst[192 + 64 * c : 256 + 64 * c, to] = along[c]
            dst[384 + 64 * c : 448 + 64 * c, to] = jnp.where(last_j, edges[c], spin(along[c], -8))


def join_layers(parts, base):
    low = lane(64, 128) < 64

    def col(a, v):
        v = v % 5
        return parts[64 * a : 64 * a + 64, base + 128 * v : base + 128 * v + 128]

    cols = []
    for v in range(4):
        mixed = jnp.where(low, col(0, v) + col(2, v + 1), col(0, v - 1) + col(2, v))
        cols.append((col(1, v) + spin(mixed, 64)).astype(BF))
    return cols


def main_kernel(
    core_ref, live_ref, nb_ref, feat_ref, grad_ref, r0, r1, r2, r3, wf_ref, wb_ref,
    out_ref, gf_ref, keep_ref, give_ref,
    cubes, xface, yface, xw, gw, gs, acc,
):
    p = pl.program_id(0)

    @pl.when(p == 0)
    def _():
        fill_tables(live_ref, feat_ref, grad_ref, r0, r1, r2, r3, cubes, xface, yface)
        acc[...] = jnp.zeros_like(acc)

    low = lane(64, 128) < 64
    zero = jnp.zeros((64, 128), BF)
    for h in range(2):
        fill_windows(0, 2 * p + h, nb_ref, cubes, xface, yface, xw, WIDE * h)
    for h in range(2):
        fill_windows(1, 2 * p + h, nb_ref, cubes, xface, yface, gw, WIDE * h)
        base = WIDE * h
        turned = [spin(cubes[1, 2 * p + h, :, 128 * v : 128 * v + 128], 64) for v in range(4)]
        for v in range(5):
            at = slice(base + 128 * v, base + 128 * v + 128)
            here = turned[v] if v < 4 else zero
            left = turned[v - 1] if v > 0 else zero
            right = turned[(v + 1) % 5] if v != 3 else zero
            gs[0:64, at] = jnp.where(low, here, right)
            gs[64:128, at] = cubes[1, 2 * p + h, :, 128 * v : 128 * v + 128] if v < 4 else zero
            gs[128:192, at] = jnp.where(low, left, here)
    acc[...] += lax.dot_general(
        gs[...], xw[...], (((1,), (1,)), ((), ())), preferred_element_type=F32
    )
    for w_ref, win, o_ref in ((wf_ref, xw, out_ref), (wb_ref, gw, gf_ref)):
        parts = jnp.dot(w_ref[...], win[...], preferred_element_type=F32)
        for h in range(2):
            alive = 2 * p + h < live_ref[0]
            for v, value in enumerate(join_layers(parts, WIDE * h)):
                o_ref[h, :, 128 * v : 128 * v + 128] = jnp.where(alive, value, zero)

    @pl.when(p == pl.num_programs(0) - 1)
    def _():
        def write(first, second):
            for t in range(128):
                ref = first if t < 64 else second
                r, q = t // 5, t % 5
                if t >= 120:
                    ref[t % 64] = jnp.zeros((8, 128), F32)
                elif q < 4:
                    ref[t % 64] = acc[8 * r : 8 * r + 8, 128 * q : 128 * q + 128]
                else:
                    ref[t % 64] = jnp.concatenate(
                        [acc[8 * r : 8 * r + 8, 512:576], jnp.zeros((8, 64), F32)], 1
                    )

        pl.when(core_ref[0] == 0)(lambda: write(keep_ref, give_ref))
        pl.when(core_ref[0] != 0)(lambda: write(give_ref, keep_ref))


def spread_kernel(scale, core_ref, own_ref, other_ref, out_ref):
    def write(first, second):
        for t in range(120):
            ref = first if t < 64 else second
            r, q = t // 5, t % 5
            a, co = r // 8, r % 8 * 8
            tile = ref[t % 64] * scale
            for half in range(2 if q < 4 else 1):
                out_ref[9 * a + 2 * q + half, co : co + 8, :] = tile[:, 64 * half : 64 * half + 64]

    pl.when(core_ref[0] == 0)(lambda: write(own_ref, other_ref))
    pl.when(core_ref[0] != 0)(lambda: write(other_ref, own_ref))


def body(features, grad_out, weights, live_count, neighbor, send_list):
    params = pltpu.CompilerParams(vmem_limit_bytes=50 * 1024 * 1024)
    face = jax.ShapeDtypeStruct((CAP, 64, 128), BF)
    o0, o1, o2, o3 = pl.pallas_call(
        faces_kernel,
        out_shape=(face,) * 4,
        in_specs=[SMEM_SPEC, VMEM_SPEC, VMEM_SPEC],
        out_specs=(VMEM_SPEC,) * 4,
        compiler_params=params,
        name="faces",
    )(send_list, features, grad_out)
    n_rows = lax.axis_size("z") * lax.axis_size("c")
    n_cols = lax.axis_size("ry")
    up_x = [(i, i + 1) for i in range(n_rows - 1)]
    down_x = [(i + 1, i) for i in range(n_rows - 1)]
    up_y = [(i, i + 1) for i in range(n_cols - 1)]
    down_y = [(i + 1, i) for i in range(n_cols - 1)]
    r0 = lax.ppermute(o1, ("z", "c"), up_x)
    r1 = lax.ppermute(o0, ("z", "c"), down_x)
    r2 = lax.ppermute(o3, "ry", up_y)
    r3 = lax.ppermute(o2, "ry", down_y)
    by_a = weights.reshape(3, 9, 64, 64)
    wf = by_a.transpose(0, 2, 1, 3).reshape(192, 576)
    wb = weights[::-1].reshape(3, 9, 64, 64).transpose(0, 3, 1, 2).reshape(192, 576)
    core = lax.axis_index("c").astype(jnp.int32).reshape(1)
    pair = pl.BlockSpec((2, 64, CELLS), lambda p: (p, 0, 0))
    half = jax.ShapeDtypeStruct((64, 8, 128), F32)
    output, grad_features, keep, give = pl.pallas_call(
        main_kernel,
        grid=(SLOTS // 2,),
        out_shape=(
            jax.ShapeDtypeStruct((SLOTS, 64, CELLS), BF),
            jax.ShapeDtypeStruct((SLOTS, 64, CELLS), BF),
            half,
            half,
        ),
        in_specs=[SMEM_SPEC] * 3 + [VMEM_SPEC] * 8,
        out_specs=(pair, pair, VMEM_SPEC, VMEM_SPEC),
        scratch_shapes=[
            pltpu.VMEM((2, SLOTS + 1, 64, CELLS), BF),
            pltpu.VMEM((2, 2, NONE + 1, 64, 128), BF),
            pltpu.VMEM((2, 2, NONE + 1, 64, CELLS), BF),
            pltpu.VMEM((576, 2 * WIDE), BF),
            pltpu.VMEM((576, 2 * WIDE), BF),
            pltpu.VMEM((192, 2 * WIDE), BF),
            pltpu.VMEM((192, 576), F32),
        ],
        compiler_params=params,
        name="convolve",
    )(core, live_count, neighbor, features, grad_out, r0, r1, r2, r3, wf, wb)
    swap = [(0, 1), (1, 0)]
    mine = keep + lax.ppermute(give, "c", swap)
    terms = lax.all_to_all(mine, ("z", "ry"), 0, 0, tiled=True)
    total = jnp.sum(terms, axis=0, keepdims=True)
    own = lax.all_to_all(
        jnp.broadcast_to(total, (64, 8, 128)), ("z", "ry"), 0, 0, tiled=True
    )
    other = lax.ppermute(own, "c", swap)
    devices = n_rows * n_cols
    scale = (512.0 * SLOTS * devices) ** (-0.5)
    grad_weights = pl.pallas_call(
        lambda *refs: spread_kernel(scale, *refs),
        out_shape=jax.ShapeDtypeStruct((27, 64, 64), F32),
        in_specs=[SMEM_SPEC, VMEM_SPEC, VMEM_SPEC],
        out_specs=VMEM_SPEC,
        compiler_params=params,
        name="spread",
    )(core, own, other)
    return output, grad_features, grad_weights


def solution(mesh):
    split = Mesh(mesh.devices.reshape(4, 2, 16), ("z", "c", "ry"))
    rows = P(("z", "c", "ry"))
    return jax.shard_map(
        body,
        mesh=split,
        in_specs=(rows, rows, P(), rows, rows, rows),
        out_specs=(rows, rows, P()),
        check_vma=False,
    )
```

```python
import jax
import jax.numpy as jnp
from jax import lax
from jax.experimental import pallas as pl
from jax.experimental.pallas import tpu as pltpu
from jax.sharding import Mesh
from jax.sharding import PartitionSpec as P

BF = jnp.bfloat16
F32 = jnp.float32
VMEM_SPEC = pl.BlockSpec(memory_space=pltpu.VMEM)
SMEM_SPEC = pl.BlockSpec(memory_space=pltpu.SMEM)
SLOTS = 8
CAP = 4
NONE = SLOTS + 2 * CAP
CELLS = 512
WIDE = 640
CORNER = {(0, 0): 55, (2, 0): 63, (0, 2): 0, (2, 2): 8}
HBM_SPEC = pl.BlockSpec(memory_space=pltpu.HBM)


def lane(rows, cols):
    return lax.broadcasted_iota(jnp.int32, (rows, cols), 1)


def spin(x, amount):
    return pltpu.roll(x, amount % 128, 1)


def column(x, v):
    return x[:, 128 * v : 128 * v + 128]


def faces_kernel(par_ref, send_hbm, feat_hbm, grad_hbm, a_ref, b_ref, c_ref, d_ref, send_ref, feat_ref, grad_ref, sems):
    copies = [pltpu.make_async_copy(send_hbm, send_ref, sems.at[0])]
    for e in range(SLOTS):
        copies.append(pltpu.make_async_copy(feat_hbm.at[e], feat_ref.at[e], sems.at[1 + e]))
        copies.append(pltpu.make_async_copy(grad_hbm.at[e], grad_ref.at[e], sems.at[9 + e]))
    for copy in copies:
        copy.start()
    low = lane(64, 128) < 64
    zero = jnp.zeros((64, 128), BF)
    cell = lax.broadcasted_iota(jnp.int32, (CELLS, 128), 0)
    spot = lane(CELLS, 128)
    same = (cell // 64 == spot // 8 % 8) & (cell % 8 == spot % 8)
    for copy in copies:
        copy.wait()

    def give_low(ref):
        for k in range(CAP):
            e = send_ref[0, k]
            s = jnp.maximum(e, 0)
            v = jnp.where(low, feat_ref[s, :, 0:128], spin(grad_ref[s, :, 0:128], 64))
            ref[k] = jnp.where(e >= 0, v, zero)

    def give_high(ref):
        for k in range(CAP):
            e = send_ref[1, k]
            s = jnp.maximum(e, 0)
            v = jnp.where(low, spin(feat_ref[s, :, 384:512], 64), grad_ref[s, :, 384:512])
            ref[k] = jnp.where(e >= 0, v, zero)

    @pl.when(par_ref[0] == 0)
    def _():
        give_high(a_ref)
        give_low(b_ref)

    @pl.when(par_ref[0] != 0)
    def _():
        give_low(a_ref)
        give_high(b_ref)

    for ref, t in ((c_ref, 3 - par_ref[1]), (d_ref, 2 + par_ref[1])):
        on = same & (cell // 8 % 8 == 7 * (t - 2))
        pick_feat = jnp.where(on & (spot < 64), 1.0, 0.0).astype(BF)
        pick_grad = jnp.where(on & (spot >= 64), 1.0, 0.0).astype(BF)
        slot = [send_ref[t, k] for k in range(CAP)]
        feats = jnp.concatenate([feat_ref[jnp.maximum(e, 0)] for e in slot], 0)
        grads = jnp.concatenate([grad_ref[jnp.maximum(e, 0)] for e in slot], 0)
        both = jnp.dot(feats, pick_feat, preferred_element_type=F32) + jnp.dot(
            grads, pick_grad, preferred_element_type=F32
        )
        both = both.astype(BF)
        for k in range(CAP):
            ref[k] = jnp.where(slot[k] >= 0, both[64 * k : 64 * k + 64], zero)


def fill_tables(n, par_ref, live_ref, ref, got, cubes, xface, tab):
    a_ref, b_ref, c_ref, d_ref = got
    low = lane(64, 128) < 64
    zero = jnp.zeros((64, 128), BF)

    def take_x(below, above):
        for k in range(CAP):
            u, v = below[k], above[k]
            xface[0, SLOTS + k] = jnp.where(low, zero, spin(u, 64) if n == 0 else u)
            xface[1, SLOTS + k] = jnp.where(low, v if n == 0 else spin(v, 64), zero)

    for e in range(SLOTS):
        alive = e < live_ref[0]
        cols = [jnp.where(alive, ref[e, :, 128 * v : 128 * v + 128], zero) for v in range(4)]
        for v in range(4):
            cubes[e, :, 128 * v : 128 * v + 128] = cols[v]
        xface[0, e] = jnp.where(low, zero, cols[3])
        xface[1, e] = jnp.where(low, cols[0], zero)
    for side in range(2):
        xface[side, NONE] = zero
    tab[NONE] = jnp.zeros((64, 1024), BF)
    pl.when(par_ref[0] == 0)(lambda: take_x(b_ref, a_ref))
    pl.when(par_ref[0] != 0)(lambda: take_x(a_ref, b_ref))
    source = lax.broadcasted_iota(jnp.int32, (128, 256), 0)
    spot = lane(128, 256)
    place = spot % 128
    from_z = jnp.where(place % 8 == 7, (place + 8) % 128, (place + 120) % 128)
    on_z = (source == from_z) & ((place % 8 == 7) | (place % 8 == 0))
    on_y = source == (place + 64) % 128
    move = jnp.where((on_z & (spot < 128)) | (on_y & (spot >= 128)), 1.0, 0.0).astype(BF)
    for v in range(4):
        many = cubes[0:SLOTS, :, 128 * v : 128 * v + 128].reshape(SLOTS * 64, 128)
        moved = jnp.dot(many, move, preferred_element_type=F32).astype(BF)
        for e in range(SLOTS):
            tab[e, :, 256 * v : 256 * v + 256] = moved[64 * e : 64 * e + 64]
    source = lax.broadcasted_iota(jnp.int32, (128, CELLS), 0)
    cell = lane(128, CELLS)
    layer = cell // 128 * 2 + 1 - cell // 64 % 2
    same = (layer == source // 8 % 8) & (cell % 8 == source % 8) & (source // 64 == n)
    for got_ref, side in ((c_ref, 1 - par_ref[1]), (d_ref, par_ref[1])):
        put = jnp.where(same & (cell // 8 % 8 == 7 * (1 - side)), 1.0, 0.0).astype(BF)
        packed = got_ref[...].reshape(CAP * 64, 128)
        full = jnp.dot(packed, put, preferred_element_type=F32).astype(BF)

        def keep(offset):
            for k in range(CAP):
                for v in range(4):
                    at = slice(256 * v + 128, 256 * v + 256)
                    tab[SLOTS + offset + k, :, at] = full[
                        64 * k : 64 * k + 64, 128 * v : 128 * v + 128
                    ]

        pl.when(side == 0)(lambda: keep(0))
        pl.when(side != 0)(lambda: keep(CAP))


def fill_windows(g, nb_ref, cubes, xface, tab, dst, base):
    def slot(side, step):
        e = nb_ref[g, side]
        near = jnp.minimum(e, SLOTS - 1)
        far = SLOTS + step + ((e - SLOTS) & (CAP - 1))
        return jnp.where(e < 0, NONE, jnp.where(e < SLOTS, near, far))

    i0, i1 = slot(0, 0), slot(1, 0)
    i2, i3 = slot(2, 0), slot(3, CAP)
    i4, i5 = slot(4, 0), slot(5, 0)
    spots = lane(64, 128)
    plane = spots % 64
    zero = jnp.zeros((64, 128), BF)
    for v in range(5):
        if v < 4:
            at = slice(256 * v, 256 * v + 128)
            up = slice(256 * v + 128, 256 * v + 256)
            mid = cubes[g, :, 128 * v : 128 * v + 128]
            rows = (
                jnp.where(plane // 8 == 7, tab[i2, :, up], mid),
                mid,
                jnp.where(plane // 8 == 0, tab[i3, :, up], mid),
            )
            ends = (tab[i4, :, at], None, tab[i5, :, at])
        else:
            mid = xface[0, i0] + xface[1, i1]
            rows = (
                jnp.where(plane // 8 == 7, zero, mid),
                mid,
                jnp.where(plane // 8 == 0, zero, mid),
            )
            ends = (zero, None, zero)
        for b in range(3):
            for c in range(3):
                x = rows[b]
                if c != 1:
                    z = ends[c]
                    if b != 1 and v < 4:
                        z = jnp.where(plane == CORNER[b, c], zero, z)
                    x = jnp.where(plane % 8 == (7 if c == 0 else 0), z, x)
                shift = 8 * (b - 1) + c - 1
                if shift:
                    x = spin(x, -shift)
                row = 64 * (3 * b + c)
                dst[row : row + 64, base + 128 * v : base + 128 * v + 128] = x


def join_layers(parts, base):
    low = lane(64, 128) < 64

    def col(a, v):
        v = v % 5
        return parts[64 * a : 64 * a + 64, base + 128 * v : base + 128 * v + 128]

    cols = []
    for v in range(4):
        mixed = jnp.where(low, col(0, v) + col(2, v + 1), col(0, v - 1) + col(2, v))
        cols.append((col(1, v) + spin(mixed, 64)).astype(BF))
    return cols


def kernel_grad_kernel(
    par_ref, live_ref, nb_ref, feat_ref, grad_ref, a_ref, b_ref, c_ref, d_ref,
    keep_ref, give_ref, cubes, xface, tab, wins, shifted, acc,
):
    low = lane(64, 128) < 64
    zero = jnp.zeros((64, 128), BF)
    got = (a_ref, b_ref, c_ref, d_ref)
    fill_tables(0, par_ref, live_ref, feat_ref, got, cubes, xface, tab)
    for p in range(SLOTS // 2):
        win, gs = wins.at[p % 2], shifted.at[p % 2]
        for h in range(2):
            g = 2 * p + h
            fill_windows(g, nb_ref, cubes, xface, tab, win, WIDE * h)
            alive = g < live_ref[0]
            cols = [
                jnp.where(alive, grad_ref[g, :, 128 * v : 128 * v + 128], zero) for v in range(4)
            ]
            turned = [spin(x, 64) for x in cols]
            for v in range(5):
                at = slice(WIDE * h + 128 * v, WIDE * h + 128 * v + 128)
                here = turned[v] if v < 4 else zero
                left = turned[v - 1] if v > 0 else zero
                right = zero if v == 3 else turned[(v + 1) % 5]
                gs[0:64, at] = jnp.where(low, here, right)
                gs[64:128, at] = cols[v] if v < 4 else zero
                gs[128:192, at] = jnp.where(low, left, here)
        part = lax.dot_general(
            gs[...], win[...], (((1,), (1,)), ((), ())), preferred_element_type=F32
        )
        if p == 0:
            acc[...] = part
        else:
            acc[...] += part

    def write(first, second):
        for t in range(128):
            ref = first if t < 64 else second
            r, q = t // 5, t % 5
            if t >= 120:
                ref[t % 64] = jnp.zeros((8, 128), F32)
            elif q < 4:
                ref[t % 64] = acc[8 * r : 8 * r + 8, 128 * q : 128 * q + 128]
            else:
                ref[t % 64] = jnp.concatenate(
                    [acc[8 * r : 8 * r + 8, 512:576], jnp.zeros((8, 64), F32)], 1
                )

    pl.when(par_ref[0] == 0)(lambda: write(keep_ref, give_ref))
    pl.when(par_ref[0] != 0)(lambda: write(give_ref, keep_ref))


def conv_kernel(
    n, par_ref, live_ref, nb_ref, cube_ref, a_ref, b_ref, c_ref, d_ref, w_ref,
    out_ref, cubes, xface, tab, win,
):
    p = pl.program_id(0)
    zero = jnp.zeros((64, 128), BF)

    @pl.when(p == 0)
    def _():
        got = (a_ref, b_ref, c_ref, d_ref)
        fill_tables(n, par_ref, live_ref, cube_ref, got, cubes, xface, tab)

    for h in range(2):
        fill_windows(2 * p + h, nb_ref, cubes, xface, tab, win, WIDE * h)
    parts = jnp.dot(w_ref[...], win[...], preferred_element_type=F32)
    for h in range(2):
        alive = 2 * p + h < live_ref[0]
        for v, value in enumerate(join_layers(parts, WIDE * h)):
            out_ref[h, :, 128 * v : 128 * v + 128] = jnp.where(alive, value, zero)


def spread_kernel(scale, total_ref, out_ref):
    for t in range(120):
        r, q = t // 5, t % 5
        a, co = r // 8, r % 8 * 8
        spot = (t % 64 // 16 * 2 + t // 64) * 16 + t % 16
        tile = total_ref[spot].astype(F32) * scale
        for half in range(2 if q < 4 else 1):
            out_ref[9 * a + 2 * q + half, co : co + 8, :] = tile[:, 64 * half : 64 * half + 64]


def swaps(count, first):
    pairs = [(i, (i + 1) % count) for i in range(first, count + first, 2)]
    return pairs + [(j, i) for i, j in pairs]


def body(features, grad_out, weights, live_count, neighbor, send_list):
    params = pltpu.CompilerParams(vmem_limit_bytes=50 * 1024 * 1024)
    n_rows = lax.axis_size("z") * lax.axis_size("c")
    n_cols = lax.axis_size("ry")
    par = jnp.stack([lax.axis_index("c"), lax.axis_index("ry") % 2]).astype(jnp.int32)
    face = jax.ShapeDtypeStruct((CAP, 64, 128), BF)
    give_a, give_b, give_c, give_d = pl.pallas_call(
        faces_kernel,
        out_shape=(face,) * 4,
        in_specs=[SMEM_SPEC, HBM_SPEC, HBM_SPEC, HBM_SPEC],
        out_specs=(VMEM_SPEC,) * 4,
        scratch_shapes=[
            pltpu.SMEM((4, CAP), jnp.int32),
            pltpu.VMEM((SLOTS, 64, CELLS), BF),
            pltpu.VMEM((SLOTS, 64, CELLS), BF),
            pltpu.SemaphoreType.DMA((17,)),
        ],
        compiler_params=pltpu.CompilerParams(vmem_limit_bytes=60 * 1024 * 1024),
        name="faces",
    )(par, send_list, features, grad_out)
    got = (
        lax.ppermute(give_a, ("z", "c"), swaps(n_rows, 0)),
        lax.ppermute(give_b, ("z", "c"), swaps(n_rows, 1)),
        lax.ppermute(give_c, "ry", swaps(n_cols, 0)),
        lax.ppermute(give_d, "ry", swaps(n_cols, 1)),
    )
    wf = weights.reshape(3, 9, 64, 64).transpose(0, 2, 1, 3).reshape(192, 576)
    wb = weights[::-1].reshape(3, 9, 64, 64).transpose(0, 3, 1, 2).reshape(192, 576)
    got, wf, wb = lax.optimization_barrier((got, wf, wb))
    tables = [
        pltpu.VMEM((SLOTS + 1, 64, CELLS), BF),
        pltpu.VMEM((2, NONE + 1, 64, 128), BF),
        pltpu.VMEM((NONE + 1, 64, 1024), BF),
    ]
    half = jax.ShapeDtypeStruct((64, 8, 128), F32)
    flops = 2 * 192 * 576 * SLOTS * WIDE
    cost = pl.CostEstimate(flops=2 * flops, bytes_accessed=8 << 20, transcendentals=0)
    keep, give = pl.pallas_call(
        kernel_grad_kernel,
        out_shape=(half, half),
        in_specs=[SMEM_SPEC] * 3 + [VMEM_SPEC] * 6,
        out_specs=(VMEM_SPEC, VMEM_SPEC),
        scratch_shapes=tables
        + [
            pltpu.VMEM((2, 576, 2 * WIDE), BF),
            pltpu.VMEM((2, 192, 2 * WIDE), BF),
            pltpu.VMEM((192, 576), F32),
        ],
        compiler_params=params,
        cost_estimate=cost,
        name="kernel_grad",
    )(par, live_count, neighbor, features, grad_out, *got)
    pair = pl.BlockSpec((2, 64, CELLS), lambda p: (p, 0, 0))

    def convolve(n, cubes, w, name):
        return pl.pallas_call(
            lambda *refs: conv_kernel(n, *refs),
            grid=(SLOTS // 2,),
            out_shape=jax.ShapeDtypeStruct((SLOTS, 64, CELLS), BF),
            in_specs=[SMEM_SPEC] * 3 + [VMEM_SPEC] * 6,
            out_specs=pair,
            scratch_shapes=tables + [pltpu.VMEM((576, 2 * WIDE), BF)],
            compiler_params=params,
            cost_estimate=cost,
            name=name,
        )(par, live_count, neighbor, cubes, *got, w)

    output = convolve(0, features, wf, "forward")
    grad_features = convolve(1, grad_out, wb, "input_grad")
    mine = keep + lax.ppermute(give, "c", [(0, 1), (1, 0)])
    terms = lax.all_to_all(mine, ("z", "ry"), 0, 0, tiled=True)
    total = jnp.sum(terms, axis=0, keepdims=True).astype(BF)
    total, output = lax.optimization_barrier((total, output))
    spread = jnp.broadcast_to(total, (n_rows * n_cols, 8, 128))
    totals = lax.all_to_all(spread, ("z", "c", "ry"), 0, 0, tiled=True)
    scale = (512.0 * SLOTS * n_rows * n_cols) ** (-0.5)
    grad_weights = pl.pallas_call(
        lambda *refs: spread_kernel(scale, *refs),
        out_shape=jax.ShapeDtypeStruct((27, 64, 64), F32),
        in_specs=[VMEM_SPEC],
        out_specs=VMEM_SPEC,
        compiler_params=params,
        name="spread",
    )(totals)
    return output, grad_features, grad_weights


def solution(mesh):
    split = Mesh(mesh.devices.reshape(4, 2, 16), ("z", "c", "ry"))
    rows = P(("z", "c", "ry"))
    return jax.shard_map(
        body,
        mesh=split,
        in_specs=(rows, rows, P(), rows, rows, rows),
        out_specs=(rows, rows, P()),
        check_vma=False,
    )
```

```python
import jax
import jax.numpy as jnp
from jax import lax
from jax.experimental import pallas as pl
from jax.experimental.pallas import tpu as pltpu
from jax.sharding import Mesh
from jax.sharding import PartitionSpec as P

BF = jnp.bfloat16
F32 = jnp.float32
VMEM_SPEC = pl.BlockSpec(memory_space=pltpu.VMEM)
SMEM_SPEC = pl.BlockSpec(memory_space=pltpu.SMEM)
SLOTS = 8
CAP = 4
NONE = SLOTS + 2 * CAP
CELLS = 512
WIDE = 640
CORNER = {(0, 0): 55, (2, 0): 63, (0, 2): 0, (2, 2): 8}
HBM_SPEC = pl.BlockSpec(memory_space=pltpu.HBM)


def lane(rows, cols):
    return lax.broadcasted_iota(jnp.int32, (rows, cols), 1)


def spin(x, amount):
    return pltpu.roll(x, amount % 128, 1)


def column(x, v):
    return x[:, 128 * v : 128 * v + 128]


def faces_kernel(
    send_hbm, feat_hbm, grad_hbm, d_ref, c_ref, b_ref, a_ref, send_ref, feat_ref, grad_ref, sems
):
    copies = [pltpu.make_async_copy(send_hbm, send_ref, sems.at[0])]
    for e in range(SLOTS):
        copies.append(pltpu.make_async_copy(feat_hbm.at[e], feat_ref.at[e], sems.at[1 + e]))
        copies.append(pltpu.make_async_copy(grad_hbm.at[e], grad_ref.at[e], sems.at[9 + e]))
    for copy in copies:
        copy.start()
    low = lane(64, 128) < 64
    zero = jnp.zeros((64, 128), BF)
    cell = lax.broadcasted_iota(jnp.int32, (CELLS, 128), 0)
    spot = lane(CELLS, 128)
    same = (cell // 64 == spot // 8 % 8) & (cell % 8 == spot % 8)
    for copy in copies:
        copy.wait()

    def give_low(ref):
        for k in range(CAP):
            e = send_ref[0, k]
            s = jnp.maximum(e, 0)
            v = jnp.where(low, feat_ref[s, :, 0:128], spin(grad_ref[s, :, 0:128], 64))
            ref[k] = jnp.where(e >= 0, v, zero)

    def give_high(ref):
        for k in range(CAP):
            e = send_ref[1, k]
            s = jnp.maximum(e, 0)
            v = jnp.where(low, spin(feat_ref[s, :, 384:512], 64), grad_ref[s, :, 384:512])
            ref[k] = jnp.where(e >= 0, v, zero)

    @pl.when(lax.axis_index("c") == 0)
    def _():
        give_high(a_ref)
        give_low(b_ref)

    @pl.when(lax.axis_index("c") != 0)
    def _():
        give_low(a_ref)
        give_high(b_ref)

    odd = lax.axis_index("ry") % 2
    for ref, t in ((c_ref, 3 - odd), (d_ref, 2 + odd)):
        on = same & (cell // 8 % 8 == 7 * (t - 2))
        pick_feat = jnp.where(on & (spot < 64), 1.0, 0.0).astype(BF)
        pick_grad = jnp.where(on & (spot >= 64), 1.0, 0.0).astype(BF)
        slot = [send_ref[t, k] for k in range(CAP)]
        feats = jnp.concatenate([feat_ref[jnp.maximum(e, 0)] for e in slot], 0)
        grads = jnp.concatenate([grad_ref[jnp.maximum(e, 0)] for e in slot], 0)
        both = jnp.dot(feats, pick_feat, preferred_element_type=F32) + jnp.dot(
            grads, pick_grad, preferred_element_type=F32
        )
        both = both.astype(BF)
        for k in range(CAP):
            ref[k] = jnp.where(slot[k] >= 0, both[64 * k : 64 * k + 64], zero)


def fill_tables(n, live_ref, ref, got, cubes, xface, tab):
    a_ref, b_ref, c_ref, d_ref = got
    low = lane(64, 128) < 64
    zero = jnp.zeros((64, 128), BF)

    def take_x(below, above):
        for k in range(CAP):
            u, v = below[k], above[k]
            xface[0, SLOTS + k] = jnp.where(low, zero, spin(u, 64) if n == 0 else u)
            xface[1, SLOTS + k] = jnp.where(low, v if n == 0 else spin(v, 64), zero)

    for e in range(SLOTS):
        alive = e < live_ref[0]
        cols = [jnp.where(alive, ref[e, :, 128 * v : 128 * v + 128], zero) for v in range(4)]
        for v in range(4):
            cubes[e, :, 128 * v : 128 * v + 128] = cols[v]
        xface[0, e] = jnp.where(low, zero, cols[3])
        xface[1, e] = jnp.where(low, cols[0], zero)
    for side in range(2):
        xface[side, NONE] = zero
    tab[NONE] = jnp.zeros((64, 1024), BF)
    pl.when(lax.axis_index("c") == 0)(lambda: take_x(b_ref, a_ref))
    pl.when(lax.axis_index("c") != 0)(lambda: take_x(a_ref, b_ref))
    source = lax.broadcasted_iota(jnp.int32, (128, 256), 0)
    spot = lane(128, 256)
    place = spot % 128
    from_z = jnp.where(place % 8 == 7, (place + 8) % 128, (place + 120) % 128)
    on_z = (source == from_z) & ((place % 8 == 7) | (place % 8 == 0))
    on_y = source == (place + 64) % 128
    move = jnp.where((on_z & (spot < 128)) | (on_y & (spot >= 128)), 1.0, 0.0).astype(BF)
    for v in range(4):
        many = cubes[0:SLOTS, :, 128 * v : 128 * v + 128].reshape(SLOTS * 64, 128)
        moved = jnp.dot(many, move, preferred_element_type=F32).astype(BF)
        for e in range(SLOTS):
            tab[e, :, 256 * v : 256 * v + 256] = moved[64 * e : 64 * e + 64]
    source = lax.broadcasted_iota(jnp.int32, (128, CELLS), 0)
    cell = lane(128, CELLS)
    layer = cell // 128 * 2 + 1 - cell // 64 % 2
    same = (layer == source // 8 % 8) & (cell % 8 == source % 8) & (source // 64 == n)
    odd = lax.axis_index("ry") % 2
    for got_ref, side in ((c_ref, 1 - odd), (d_ref, odd)):
        put = jnp.where(same & (cell // 8 % 8 == 7 * (1 - side)), 1.0, 0.0).astype(BF)
        packed = got_ref[...].reshape(CAP * 64, 128)
        full = jnp.dot(packed, put, preferred_element_type=F32).astype(BF)

        def keep(offset):
            for k in range(CAP):
                for v in range(4):
                    at = slice(256 * v + 128, 256 * v + 256)
                    tab[SLOTS + offset + k, :, at] = full[
                        64 * k : 64 * k + 64, 128 * v : 128 * v + 128
                    ]

        pl.when(side == 0)(lambda: keep(0))
        pl.when(side != 0)(lambda: keep(CAP))


def fill_windows(g, nb_ref, cubes, xface, tab, dst, base):
    def slot(side, step):
        e = nb_ref[g, side]
        near = jnp.minimum(e, SLOTS - 1)
        far = SLOTS + step + ((e - SLOTS) & (CAP - 1))
        return jnp.where(e < 0, NONE, jnp.where(e < SLOTS, near, far))

    i0, i1 = slot(0, 0), slot(1, 0)
    i2, i3 = slot(2, 0), slot(3, CAP)
    i4, i5 = slot(4, 0), slot(5, 0)
    spots = lane(64, 128)
    plane = spots % 64
    zero = jnp.zeros((64, 128), BF)
    for v in range(5):
        if v < 4:
            at = slice(256 * v, 256 * v + 128)
            up = slice(256 * v + 128, 256 * v + 256)
            mid = cubes[g, :, 128 * v : 128 * v + 128]
            rows = (
                jnp.where(plane // 8 == 7, tab[i2, :, up], mid),
                mid,
                jnp.where(plane // 8 == 0, tab[i3, :, up], mid),
            )
            ends = (tab[i4, :, at], None, tab[i5, :, at])
        else:
            mid = xface[0, i0] + xface[1, i1]
            rows = (
                jnp.where(plane // 8 == 7, zero, mid),
                mid,
                jnp.where(plane // 8 == 0, zero, mid),
            )
            ends = (zero, None, zero)
        for b in range(3):
            for c in range(3):
                x = rows[b]
                if c != 1:
                    z = ends[c]
                    if b != 1 and v < 4:
                        z = jnp.where(plane == CORNER[b, c], zero, z)
                    x = jnp.where(plane % 8 == (7 if c == 0 else 0), z, x)
                shift = 8 * (b - 1) + c - 1
                if shift:
                    x = spin(x, -shift)
                row = 64 * (3 * b + c)
                dst[row : row + 64, base + 128 * v : base + 128 * v + 128] = x


def join_layers(parts, base):
    low = lane(64, 128) < 64

    def col(a, v):
        v = v % 5
        return parts[64 * a : 64 * a + 64, base + 128 * v : base + 128 * v + 128]

    cols = []
    for v in range(4):
        mixed = jnp.where(low, col(0, v) + col(2, v + 1), col(0, v - 1) + col(2, v))
        cols.append((col(1, v) + spin(mixed, 64)).astype(BF))
    return cols


def kernel_grad_kernel(
    live_ref, nb_ref, feat_ref, grad_ref, d_ref, c_ref, b_ref, a_ref,
    keep_ref, give_ref, cubes, xface, tab, wins, shifted, acc,
):
    low = lane(64, 128) < 64
    zero = jnp.zeros((64, 128), BF)
    got = (a_ref, b_ref, c_ref, d_ref)
    fill_tables(0, live_ref, feat_ref, got, cubes, xface, tab)
    for p in range(SLOTS // 2):
        win, gs = wins.at[p % 2], shifted.at[p % 2]
        for h in range(2):
            g = 2 * p + h
            fill_windows(g, nb_ref, cubes, xface, tab, win, WIDE * h)
            alive = g < live_ref[0]
            cols = [
                jnp.where(alive, grad_ref[g, :, 128 * v : 128 * v + 128], zero) for v in range(4)
            ]
            turned = [spin(x, 64) for x in cols]
            for v in range(5):
                at = slice(WIDE * h + 128 * v, WIDE * h + 128 * v + 128)
                here = turned[v] if v < 4 else zero
                left = turned[v - 1] if v > 0 else zero
                right = zero if v == 3 else turned[(v + 1) % 5]
                gs[0:64, at] = jnp.where(low, here, right)
                gs[64:128, at] = cols[v] if v < 4 else zero
                gs[128:192, at] = jnp.where(low, left, here)
        part = lax.dot_general(
            gs[...], win[...], (((1,), (1,)), ((), ())), preferred_element_type=F32
        )
        if p == 0:
            acc[...] = part
        else:
            acc[...] += part

    def write(first, second):
        for t in range(128):
            ref = first if t < 64 else second
            r, q = t // 5, t % 5
            if t >= 120:
                ref[t % 64] = jnp.zeros((8, 128), F32)
            elif q < 4:
                ref[t % 64] = acc[8 * r : 8 * r + 8, 128 * q : 128 * q + 128]
            else:
                ref[t % 64] = jnp.concatenate(
                    [acc[8 * r : 8 * r + 8, 512:576], jnp.zeros((8, 64), F32)], 1
                )

    pl.when(lax.axis_index("c") == 0)(lambda: write(keep_ref, give_ref))
    pl.when(lax.axis_index("c") != 0)(lambda: write(give_ref, keep_ref))


def conv_kernel(
    n, live_ref, nb_ref, cube_ref, d_ref, c_ref, b_ref, a_ref, w_ref,
    out_ref, cubes, xface, tab, win,
):
    p = pl.program_id(0)
    zero = jnp.zeros((64, 128), BF)

    @pl.when(p == 0)
    def _():
        got = (a_ref, b_ref, c_ref, d_ref)
        fill_tables(n, live_ref, cube_ref, got, cubes, xface, tab)

    for h in range(2):
        fill_windows(2 * p + h, nb_ref, cubes, xface, tab, win, WIDE * h)
    parts = jnp.dot(w_ref[...], win[...], preferred_element_type=F32)
    for h in range(2):
        alive = 2 * p + h < live_ref[0]
        for v, value in enumerate(join_layers(parts, WIDE * h)):
            out_ref[h, :, 128 * v : 128 * v + 128] = jnp.where(alive, value, zero)


def spread_kernel(scale, total_ref, out_ref):
    for t in range(120):
        r, q = t // 5, t % 5
        a, co = r // 8, r % 8 * 8
        spot = (t % 64 // 16 * 2 + t // 64) * 16 + t % 16
        tile = total_ref[spot].astype(F32) * scale
        for half in range(2 if q < 4 else 1):
            out_ref[9 * a + 2 * q + half, co : co + 8, :] = tile[:, 64 * half : 64 * half + 64]


def swaps(count, first):
    pairs = [(i, (i + 1) % count) for i in range(first, count + first, 2)]
    return pairs + [(j, i) for i, j in pairs]


def body(features, grad_out, weights, live_count, neighbor, send_list):
    params = pltpu.CompilerParams(vmem_limit_bytes=50 * 1024 * 1024)
    n_rows = lax.axis_size("z") * lax.axis_size("c")
    n_cols = lax.axis_size("ry")
    face = jax.ShapeDtypeStruct((CAP, 64, 128), BF)
    give_d, give_c, give_b, give_a = pl.pallas_call(
        faces_kernel,
        out_shape=(face,) * 4,
        in_specs=[HBM_SPEC, HBM_SPEC, HBM_SPEC],
        out_specs=(VMEM_SPEC,) * 4,
        scratch_shapes=[
            pltpu.SMEM((4, CAP), jnp.int32),
            pltpu.VMEM((SLOTS, 64, CELLS), BF),
            pltpu.VMEM((SLOTS, 64, CELLS), BF),
            pltpu.SemaphoreType.DMA((17,)),
        ],
        compiler_params=pltpu.CompilerParams(vmem_limit_bytes=56000000),
        name="faces",
    )(pltpu.with_memory_space_constraint(send_list, pltpu.HBM), features, grad_out)
    got_d = lax.ppermute(give_d, "ry", swaps(n_cols, 1))
    got_c = lax.ppermute(give_c, "ry", swaps(n_cols, 0))
    got_b = lax.ppermute(give_b, ("z", "c"), swaps(n_rows, 1))
    got_a = lax.ppermute(give_a, ("z", "c"), swaps(n_rows, 0))
    got = (got_d, got_c, got_b, got_a)
    wf = weights.reshape(3, 9, 64, 64).transpose(0, 2, 1, 3).reshape(192, 576)
    wb = weights[::-1].reshape(3, 9, 64, 64).transpose(0, 3, 1, 2).reshape(192, 576)
    got, wf, wb = lax.optimization_barrier((got, wf, wb))
    tables = [
        pltpu.VMEM((SLOTS + 1, 64, CELLS), BF),
        pltpu.VMEM((2, NONE + 1, 64, 128), BF),
        pltpu.VMEM((NONE + 1, 64, 1024), BF),
    ]
    half = jax.ShapeDtypeStruct((64, 8, 128), F32)
    flops = 2 * 192 * 576 * SLOTS * WIDE
    cost = pl.CostEstimate(flops=2 * flops, bytes_accessed=8 << 20, transcendentals=0)
    keep, give = pl.pallas_call(
        kernel_grad_kernel,
        out_shape=(half, half),
        in_specs=[SMEM_SPEC] * 2 + [VMEM_SPEC] * 6,
        out_specs=(VMEM_SPEC, VMEM_SPEC),
        scratch_shapes=tables
        + [
            pltpu.VMEM((2, 576, 2 * WIDE), BF),
            pltpu.VMEM((2, 192, 2 * WIDE), BF),
            pltpu.VMEM((192, 576), F32),
        ],
        compiler_params=params,
        cost_estimate=cost,
        name="kernel_grad",
    )(live_count, neighbor, features, grad_out, *got)
    pair = pl.BlockSpec((2, 64, CELLS), lambda p: (p, 0, 0))

    def convolve(n, cubes, w, name):
        return pl.pallas_call(
            lambda *refs: conv_kernel(n, *refs),
            grid=(SLOTS // 2,),
            out_shape=jax.ShapeDtypeStruct((SLOTS, 64, CELLS), BF),
            in_specs=[SMEM_SPEC] * 2 + [VMEM_SPEC] * 6,
            out_specs=pair,
            scratch_shapes=tables + [pltpu.VMEM((576, 2 * WIDE), BF)],
            compiler_params=params,
            cost_estimate=cost,
            name=name,
        )(live_count, neighbor, cubes, *got, w)

    output = convolve(0, features, wf, "forward")
    grad_features = convolve(1, grad_out, wb, "input_grad")
    mine = keep + lax.ppermute(give, "c", [(0, 1), (1, 0)])
    terms = lax.all_to_all(mine, ("z", "ry"), 0, 0, tiled=True)
    total = jnp.sum(terms, axis=0, keepdims=True).astype(BF)
    total, output = lax.optimization_barrier((total, output))
    spread = jnp.broadcast_to(total, (n_rows * n_cols, 8, 128))
    totals = lax.all_to_all(spread, ("z", "c", "ry"), 0, 0, tiled=True)
    scale = (512.0 * SLOTS * n_rows * n_cols) ** (-0.5)
    grad_weights = pl.pallas_call(
        lambda *refs: spread_kernel(scale, *refs),
        out_shape=jax.ShapeDtypeStruct((27, 64, 64), F32),
        in_specs=[VMEM_SPEC],
        out_specs=VMEM_SPEC,
        compiler_params=params,
        name="spread",
    )(totals)
    return output, grad_features, grad_weights


def solution(mesh):
    split = Mesh(mesh.devices.reshape(4, 2, 16), ("z", "c", "ry"))
    rows = P(("z", "c", "ry"))
    return jax.shard_map(
        body,
        mesh=split,
        in_specs=(rows, rows, P(), rows, rows, rows),
        out_specs=(rows, rows, P()),
        check_vma=False,
    )
```

```python
import jax
import jax.numpy as jnp
import numpy as np
from jax import lax
from jax.experimental import pallas as pl
from jax.experimental.pallas import tpu as pltpu
from jax.sharding import Mesh
from jax.sharding import PartitionSpec as P

BF = jnp.bfloat16
F32 = jnp.float32
VMEM_SPEC = pl.BlockSpec(memory_space=pltpu.VMEM)
SMEM_SPEC = pl.BlockSpec(memory_space=pltpu.SMEM)
SLOTS = 8
CAP = 4
NONE = SLOTS + 2 * CAP
CELLS = 512
WIDE = 640
CORNER = {(0, 0): 55, (2, 0): 63, (0, 2): 0, (2, 2): 8}
HBM_SPEC = pl.BlockSpec(memory_space=pltpu.HBM)


def lane(rows, cols):
    return lax.broadcasted_iota(jnp.int32, (rows, cols), 1)


def spin(x, amount):
    return pltpu.roll(x, amount % 128, 1)


def column(x, v):
    return x[:, 128 * v : 128 * v + 128]


def faces_kernel(
    send_hbm, nb_hbm, feat_hbm, grad_hbm,
    d_ref, c_ref, b_ref, a_ref, nb_ref, feat_ref, grad_ref, send_ref, sems,
):
    copies = [
        pltpu.make_async_copy(send_hbm, send_ref, sems.at[0]),
        pltpu.make_async_copy(nb_hbm, nb_ref, sems.at[17]),
    ]
    for e in range(SLOTS):
        copies.append(pltpu.make_async_copy(feat_hbm.at[e], feat_ref.at[e], sems.at[1 + e]))
        copies.append(pltpu.make_async_copy(grad_hbm.at[e], grad_ref.at[e], sems.at[9 + e]))
    for copy in copies:
        copy.start()
    low = lane(64, 128) < 64
    zero = jnp.zeros((64, 128), BF)
    cell = lax.broadcasted_iota(jnp.int32, (CELLS, 128), 0)
    spot = lane(CELLS, 128)
    same = (cell // 64 == spot // 8 % 8) & (cell % 8 == spot % 8)
    for copy in copies:
        copy.wait()

    def give_low(ref):
        for k in range(CAP):
            e = send_ref[0, k]
            s = jnp.maximum(e, 0)
            v = jnp.where(low, feat_ref[s, :, 0:128], spin(grad_ref[s, :, 0:128], 64))
            ref[k] = jnp.where(e >= 0, v, zero)

    def give_high(ref):
        for k in range(CAP):
            e = send_ref[1, k]
            s = jnp.maximum(e, 0)
            v = jnp.where(low, spin(feat_ref[s, :, 384:512], 64), grad_ref[s, :, 384:512])
            ref[k] = jnp.where(e >= 0, v, zero)

    @pl.when(lax.axis_index("c") == 0)
    def _():
        give_high(a_ref)
        give_low(b_ref)

    @pl.when(lax.axis_index("c") != 0)
    def _():
        give_low(a_ref)
        give_high(b_ref)

    odd = lax.axis_index("ry") % 2
    for ref, t in ((c_ref, 3 - odd), (d_ref, 2 + odd)):
        on = same & (cell // 8 % 8 == 7 * (t - 2))
        pick_feat = jnp.where(on & (spot < 64), 1.0, 0.0).astype(BF)
        pick_grad = jnp.where(on & (spot >= 64), 1.0, 0.0).astype(BF)
        slot = [send_ref[t, k] for k in range(CAP)]
        feats = jnp.concatenate([feat_ref[jnp.maximum(e, 0)] for e in slot], 0)
        grads = jnp.concatenate([grad_ref[jnp.maximum(e, 0)] for e in slot], 0)
        both = jnp.dot(feats, pick_feat, preferred_element_type=F32) + jnp.dot(
            grads, pick_grad, preferred_element_type=F32
        )
        both = both.astype(BF)
        for k in range(CAP):
            ref[k] = jnp.where(slot[k] >= 0, both[64 * k : 64 * k + 64], zero)


def fill_near(live_ref, ref, cubes, xface, tab):
    low = lane(64, 128) < 64
    zero = jnp.zeros((64, 128), BF)
    for e in range(SLOTS):
        alive = e < live_ref[0]
        cols = [jnp.where(alive, ref[e, :, 128 * v : 128 * v + 128], zero) for v in range(4)]
        for v in range(4):
            cubes[e, :, 128 * v : 128 * v + 128] = cols[v]
        xface[0, e] = jnp.where(low, zero, cols[3])
        xface[1, e] = jnp.where(low, cols[0], zero)
    for side in range(2):
        xface[side, NONE] = zero
    tab[NONE] = jnp.zeros((64, 1024), BF)
    source = lax.broadcasted_iota(jnp.int32, (128, 256), 0)
    spot = lane(128, 256)
    place = spot % 128
    from_z = jnp.where(place % 8 == 7, (place + 8) % 128, (place + 120) % 128)
    on_z = (source == from_z) & ((place % 8 == 7) | (place % 8 == 0))
    on_y = source == (place + 64) % 128
    move = jnp.where((on_z & (spot < 128)) | (on_y & (spot >= 128)), 1.0, 0.0).astype(BF)
    for v in range(4):
        many = cubes[0:SLOTS, :, 128 * v : 128 * v + 128].reshape(SLOTS * 64, 128)
        moved = jnp.dot(many, move, preferred_element_type=F32).astype(BF)
        for e in range(SLOTS):
            tab[e, :, 256 * v : 256 * v + 256] = moved[64 * e : 64 * e + 64]


def fill_far(n, got, xface, tab):
    d_ref, c_ref, b_ref, a_ref = got
    low = lane(64, 128) < 64
    zero = jnp.zeros((64, 128), BF)

    def take_x(below, above):
        for k in range(CAP):
            u, v = below[k], above[k]
            xface[0, SLOTS + k] = jnp.where(low, zero, spin(u, 64) if n == 0 else u)
            xface[1, SLOTS + k] = jnp.where(low, v if n == 0 else spin(v, 64), zero)

    pl.when(lax.axis_index("c") == 0)(lambda: take_x(b_ref, a_ref))
    pl.when(lax.axis_index("c") != 0)(lambda: take_x(a_ref, b_ref))
    source = lax.broadcasted_iota(jnp.int32, (128, CELLS), 0)
    cell = lane(128, CELLS)
    layer = cell // 128 * 2 + 1 - cell // 64 % 2
    same = (layer == source // 8 % 8) & (cell % 8 == source % 8) & (source // 64 == n)
    odd = lax.axis_index("ry") % 2
    for got_ref, side in ((c_ref, 1 - odd), (d_ref, odd)):
        put = jnp.where(same & (cell // 8 % 8 == 7 * (1 - side)), 1.0, 0.0).astype(BF)
        packed = got_ref[...].reshape(CAP * 64, 128)
        full = jnp.dot(packed, put, preferred_element_type=F32).astype(BF)

        def keep(offset):
            for k in range(CAP):
                for v in range(4):
                    at = slice(256 * v + 128, 256 * v + 256)
                    tab[SLOTS + offset + k, :, at] = full[
                        64 * k : 64 * k + 64, 128 * v : 128 * v + 128
                    ]

        pl.when(side == 0)(lambda: keep(0))
        pl.when(side != 0)(lambda: keep(CAP))


def fill_windows(g, far, nb_ref, cubes, xface, tab, dst, base):
    def slot(side, step):
        e = nb_ref[g, side]
        near = jnp.minimum(e, SLOTS - 1)
        away = SLOTS + step + ((e - SLOTS) & (CAP - 1)) if far else NONE
        return jnp.where(e < 0, NONE, jnp.where(e < SLOTS, near, away))

    i0, i1 = slot(0, 0), slot(1, 0)
    i2, i3 = slot(2, 0), slot(3, CAP)
    i4, i5 = slot(4, 0), slot(5, 0)
    spots = lane(64, 128)
    plane = spots % 64
    zero = jnp.zeros((64, 128), BF)
    for v in range(5):
        if v < 4:
            at = slice(256 * v, 256 * v + 128)
            up = slice(256 * v + 128, 256 * v + 256)
            mid = cubes[g, :, 128 * v : 128 * v + 128]
            rows = (
                jnp.where(plane // 8 == 7, tab[i2, :, up], mid),
                mid,
                jnp.where(plane // 8 == 0, tab[i3, :, up], mid),
            )
            ends = (tab[i4, :, at], None, tab[i5, :, at])
        else:
            mid = xface[0, i0] + xface[1, i1]
            rows = (
                jnp.where(plane // 8 == 7, zero, mid),
                mid,
                jnp.where(plane // 8 == 0, zero, mid),
            )
            ends = (zero, None, zero)
        for b in range(3):
            for c in range(3):
                x = rows[b]
                if c != 1:
                    z = ends[c]
                    if b != 1 and v < 4:
                        z = jnp.where(plane == CORNER[b, c], zero, z)
                    x = jnp.where(plane % 8 == (7 if c == 0 else 0), z, x)
                shift = 8 * (b - 1) + c - 1
                if shift:
                    x = spin(x, -shift)
                row = 64 * (3 * b + c)
                dst[row : row + 64, base + 128 * v : base + 128 * v + 128] = x


def join_layers(parts, base):
    low = lane(64, 128) < 64

    def col(a, v):
        v = v % 5
        return parts[64 * a : 64 * a + 64, base + 128 * v : base + 128 * v + 128]

    cols = []
    for v in range(4):
        mixed = jnp.where(low, col(0, v) + col(2, v + 1), col(0, v - 1) + col(2, v))
        cols.append((col(1, v) + spin(mixed, 64)).astype(BF))
    return cols


def near_kernel(live_ref, nb_ref, feat_ref, grad_ref, acc_ref, shift_ref, cubes, xface, tab, wins):
    low = lane(64, 128) < 64
    zero = jnp.zeros((64, 128), BF)
    fill_near(live_ref, feat_ref, cubes, xface, tab)
    for p in range(SLOTS // 2):
        win = wins.at[p % 2]
        for h in range(2):
            g = 2 * p + h
            fill_windows(g, False, nb_ref, cubes, xface, tab, win, WIDE * h)
            alive = g < live_ref[0]
            cols = [
                jnp.where(alive, grad_ref[g, :, 128 * v : 128 * v + 128], zero) for v in range(4)
            ]
            turned = [spin(x, 64) for x in cols]
            for v in range(5):
                at = slice(WIDE * h + 128 * v, WIDE * h + 128 * v + 128)
                here = turned[v] if v < 4 else zero
                left = turned[v - 1] if v > 0 else zero
                right = zero if v == 3 else turned[(v + 1) % 5]
                shift_ref[p, 0:64, at] = jnp.where(low, here, right)
                shift_ref[p, 64:128, at] = cols[v] if v < 4 else zero
                shift_ref[p, 128:192, at] = jnp.where(low, left, here)
        part = lax.dot_general(
            shift_ref[p], win[...], (((1,), (1,)), ((), ())), preferred_element_type=F32
        )
        if p == 0:
            acc_ref[...] = part
        else:
            acc_ref[...] += part


def face_moves():
    source = np.arange(128)[:, None]
    into_x = np.zeros((2, 128, 9 * 128), np.float32)
    into_y = np.zeros((2, 128, 3 * CELLS), np.float32)
    spot = np.arange(128)[None]
    cell = np.arange(CELLS)[None]
    for side in range(2):
        for b in range(3):
            for c in range(3):
                j, k = spot // 8 % 8 + b - 1, spot % 8 + c - 1
                inside = (j >= 0) & (j < 8) & (k >= 0) & (k < 8) & (spot // 64 == 1 - side)
                col = 128 * (3 * b + c)
                into_x[side, :, col : col + 128] = inside & (source == 8 * j + k)
        for c in range(3):
            k = cell % 8 + c - 1
            inside = (k >= 0) & (k < 8) & (cell // 8 % 8 == 7 * side)
            into_y[side, :, CELLS * c : CELLS * c + CELLS] = inside & (
                source == cell // 64 * 8 + k
            )
    return jnp.asarray(into_x, BF), jnp.asarray(into_y, BF)


def kernel_grad_kernel(
    nb_ref, near_ref, shift_ref, into_x, into_y, d_ref, c_ref, b_ref, a_ref,
    keep_ref, give_ref, xfar, yfar, ghosts, edges, acc,
):
    core = lax.axis_index("c")
    odd = lax.axis_index("ry") % 2
    for side in range(2):
        xfar[side, CAP] = jnp.zeros((576, 128), BF)
        yfar[side, CAP] = jnp.zeros((192, CELLS), BF)
    for got_ref, side, into, far, width in (
        (d_ref, odd, into_y, yfar, CELLS),
        (c_ref, 1 - odd, into_y, yfar, CELLS),
        (b_ref, core, into_x, xfar, 128),
        (a_ref, 1 - core, into_x, xfar, 128),
    ):
        packed = got_ref[...].reshape(CAP * 64, 128)
        full = jnp.dot(packed, into[side], preferred_element_type=F32).astype(BF)
        for k in range(CAP):
            for n in range(far.shape[2] // 64):
                far[side, k, 64 * n : 64 * n + 64, :] = full[
                    64 * k : 64 * k + 64, width * n : width * n + width
                ]
    rims = [None, None]
    for g in range(SLOTS):
        p, base = g // 2, WIDE * (g % 2)
        e = [nb_ref[g, side] for side in range(4)]
        i = [jnp.where(x < SLOTS, CAP, (x - SLOTS) & (CAP - 1)) for x in e]
        ghosts[:, 128 * g : 128 * g + 128] = xfar[0, i[0]] + xfar[1, i[1]]
        edges[:, 128 * g : 128 * g + 128] = shift_ref[p, :, base + 512 : base + 640]
        for side in range(2):
            part = lax.dot_general(
                shift_ref[p, :, base : base + 512],
                yfar[side, i[2 + side]],
                (((1,), (1,)), ((), ())),
                preferred_element_type=F32,
            )
            rims[side] = part if g == 0 else rims[side] + part
    acc[...] = near_ref[...] + lax.dot_general(
        edges[...], ghosts[...], (((1,), (1,)), ((), ())), preferred_element_type=F32
    )
    acc[:, 0:192] += rims[0]
    acc[:, 384:576] += rims[1]

    def write(first, second):
        for t in range(128):
            ref = first if t < 64 else second
            r, q = t // 5, t % 5
            if t >= 120:
                ref[t % 64] = jnp.zeros((8, 128), F32)
            elif q < 4:
                ref[t % 64] = acc[8 * r : 8 * r + 8, 128 * q : 128 * q + 128]
            else:
                ref[t % 64] = jnp.concatenate(
                    [acc[8 * r : 8 * r + 8, 512:576], jnp.zeros((8, 64), F32)], 1
                )

    pl.when(lax.axis_index("c") == 0)(lambda: write(keep_ref, give_ref))
    pl.when(lax.axis_index("c") != 0)(lambda: write(give_ref, keep_ref))


def conv_kernel(
    n, live_ref, nb_ref, cube_ref, d_ref, c_ref, b_ref, a_ref, w_ref,
    out_hbm, cubes, xface, tab, wins, mat, outs, sems,
):
    zero = jnp.zeros((64, 128), BF)
    eye = lax.broadcasted_iota(jnp.int32, (64, 64), 0) == lane(64, 64)
    eye = jnp.where(eye, 1.0, 0.0).astype(BF)
    for a in range(3):
        if n == 0:
            block = jnp.concatenate([w_ref[9 * a + o] for o in range(9)], axis=1)
        else:
            tall = jnp.concatenate([w_ref[26 - 9 * a - o] for o in range(9)], axis=0)
            block = lax.dot_general(
                eye, tall, (((1,), (1,)), ((), ())), preferred_element_type=F32
            ).astype(BF)
        mat[64 * a : 64 * a + 64] = block
    got = (d_ref, c_ref, b_ref, a_ref)
    fill_near(live_ref, cube_ref, cubes, xface, tab)
    fill_far(n, got, xface, tab)
    copies = []
    for p in range(SLOTS // 2):
        win = wins.at[p % 2]
        for h in range(2):
            fill_windows(2 * p + h, True, nb_ref, cubes, xface, tab, win, WIDE * h)
        parts = jnp.dot(mat[...], win[...], preferred_element_type=F32)
        for h in range(2):
            alive = 2 * p + h < live_ref[0]
            for v, value in enumerate(join_layers(parts, WIDE * h)):
                outs[2 * p + h, :, 128 * v : 128 * v + 128] = jnp.where(alive, value, zero)
        part = pl.ds(2 * p, 2)
        copies.append(pltpu.make_async_copy(outs.at[part], out_hbm.at[part], sems.at[p]))
        copies[-1].start()
    for copy in copies:
        copy.wait()


def spread_kernel(scale, total_ref, out_ref):
    for t in range(120):
        r, q = t // 5, t % 5
        a, co = r // 8, r % 8 * 8
        spot = (t % 64 // 16 * 2 + t // 64) * 16 + t % 16
        tile = total_ref[spot].astype(F32) * scale
        for half in range(2 if q < 4 else 1):
            out_ref[9 * a + 2 * q + half, co : co + 8, :] = tile[:, 64 * half : 64 * half + 64]


def swaps(count, first):
    pairs = [(i, (i + 1) % count) for i in range(first, count + first, 2)]
    return pairs + [(j, i) for i, j in pairs]


def body(features, grad_out, weights, live_count, neighbor, send_list):
    params = pltpu.CompilerParams(vmem_limit_bytes=50 * 1024 * 1024)
    n_rows = lax.axis_size("z") * lax.axis_size("c")
    n_cols = lax.axis_size("ry")
    face = jax.ShapeDtypeStruct((CAP, 64, 128), BF)
    cells = jax.ShapeDtypeStruct((SLOTS, 64, CELLS), BF)
    give_d, give_c, give_b, give_a, neighbor, features, grad_out = pl.pallas_call(
        faces_kernel,
        out_shape=(face,) * 4 + (jax.ShapeDtypeStruct((SLOTS, 6), jnp.int32), cells, cells),
        in_specs=[HBM_SPEC] * 4,
        out_specs=(VMEM_SPEC,) * 7,
        scratch_shapes=[pltpu.SMEM((4, CAP), jnp.int32), pltpu.SemaphoreType.DMA((18,))],
        compiler_params=pltpu.CompilerParams(vmem_limit_bytes=48 * 1024 * 1024),
        name="faces",
    )(*(pltpu.with_memory_space_constraint(x, pltpu.HBM) for x in (send_list, neighbor, features, grad_out)))
    got_d = lax.ppermute(give_d, "ry", swaps(n_cols, 1))
    got_c = lax.ppermute(give_c, "ry", swaps(n_cols, 0))
    got_b = lax.ppermute(give_b, ("z", "c"), swaps(n_rows, 1))
    got_a = lax.ppermute(give_a, ("z", "c"), swaps(n_rows, 0))
    got = (got_d, got_c, got_b, got_a)
    tables = [
        pltpu.VMEM((SLOTS + 1, 64, CELLS), BF),
        pltpu.VMEM((2, NONE + 1, 64, 128), BF),
        pltpu.VMEM((NONE + 1, 64, 1024), BF),
    ]
    half = jax.ShapeDtypeStruct((64, 8, 128), F32)
    flops = 2 * 192 * 576 * SLOTS * WIDE
    cost = pl.CostEstimate(flops=2 * flops, bytes_accessed=8 << 20, transcendentals=0)
    small = pltpu.CompilerParams(vmem_limit_bytes=24 * 1024 * 1024)
    near, shifted = pl.pallas_call(
        near_kernel,
        out_shape=(
            jax.ShapeDtypeStruct((192, 576), F32),
            jax.ShapeDtypeStruct((SLOTS // 2, 192, 2 * WIDE), BF),
        ),
        in_specs=[SMEM_SPEC] * 2 + [VMEM_SPEC] * 2,
        out_specs=(VMEM_SPEC, VMEM_SPEC),
        scratch_shapes=tables + [pltpu.VMEM((2, 576, 2 * WIDE), BF)],
        compiler_params=small,
        cost_estimate=cost,
        name="near_pairs",
    )(live_count, neighbor, features, grad_out)
    keep, give = pl.pallas_call(
        kernel_grad_kernel,
        out_shape=(half, half),
        in_specs=[SMEM_SPEC] + [VMEM_SPEC] * 8,
        out_specs=(VMEM_SPEC, VMEM_SPEC),
        scratch_shapes=[
            pltpu.VMEM((2, CAP + 1, 576, 128), BF),
            pltpu.VMEM((2, CAP + 1, 192, CELLS), BF),
            pltpu.VMEM((576, 128 * SLOTS), BF),
            pltpu.VMEM((192, 128 * SLOTS), BF),
            pltpu.VMEM((192, 576), F32),
        ],
        compiler_params=small,
        cost_estimate=cost,
        name="kernel_grad",
    )(neighbor, near, shifted, *face_moves(), *got)

    def convolve(n, cubes, w, name):
        return pl.pallas_call(
            lambda *refs: conv_kernel(n, *refs),
            out_shape=jax.ShapeDtypeStruct((SLOTS, 64, CELLS), BF),
            in_specs=[SMEM_SPEC] * 2 + [VMEM_SPEC] * 6,
            out_specs=HBM_SPEC,
            scratch_shapes=tables
            + [
                pltpu.VMEM((2, 576, 2 * WIDE), BF),
                pltpu.VMEM((192, 576), BF),
                pltpu.VMEM((SLOTS, 64, CELLS), BF),
                pltpu.SemaphoreType.DMA((SLOTS // 2,)),
            ],
            compiler_params=small,
            cost_estimate=cost,
            name=name,
        )(live_count, neighbor, cubes, *got, w)

    mine = keep + lax.ppermute(give, "c", [(0, 1), (1, 0)])
    output = convolve(0, features, weights, "forward")
    grad_features = convolve(1, grad_out, weights, "input_grad")
    terms = lax.all_to_all(mine, ("z", "ry"), 0, 0, tiled=True)
    total = jnp.sum(terms, axis=0, keepdims=True).astype(BF)
    total, output = lax.optimization_barrier((total, output))
    spread = jnp.broadcast_to(total, (n_rows * n_cols, 8, 128))
    totals = lax.all_to_all(spread, ("z", "c", "ry"), 0, 0, tiled=True)
    scale = (512.0 * SLOTS * n_rows * n_cols) ** (-0.5)
    grad_weights = pl.pallas_call(
        lambda *refs: spread_kernel(scale, *refs),
        out_shape=jax.ShapeDtypeStruct((27, 64, 64), F32),
        in_specs=[VMEM_SPEC],
        out_specs=VMEM_SPEC,
        compiler_params=params,
        name="spread",
    )(totals)
    return output, grad_features, grad_weights


def solution(mesh):
    split = Mesh(mesh.devices.reshape(4, 2, 16), ("z", "c", "ry"))
    rows = P(("z", "c", "ry"))
    return jax.shard_map(
        body,
        mesh=split,
        in_specs=(rows, rows, P(), rows, rows, rows),
        out_specs=(rows, rows, P()),
        check_vma=False,
    )
```

```python
import jax
import jax.numpy as jnp
import numpy as np
from jax import lax
from jax.experimental import pallas as pl
from jax.experimental.pallas import tpu as pltpu
from jax.sharding import Mesh
from jax.sharding import PartitionSpec as P

BF = jnp.bfloat16
F32 = jnp.float32
VMEM_SPEC = pl.BlockSpec(memory_space=pltpu.VMEM)
SMEM_SPEC = pl.BlockSpec(memory_space=pltpu.SMEM)
SLOTS = 8
CAP = 4
NONE = SLOTS + 2 * CAP
CELLS = 512
WIDE = 640
CORNER = {(0, 0): 55, (2, 0): 63, (0, 2): 0, (2, 2): 8}
HBM_SPEC = pl.BlockSpec(memory_space=pltpu.HBM)


def lane(rows, cols):
    return lax.broadcasted_iota(jnp.int32, (rows, cols), 1)


def spin(x, amount):
    return pltpu.roll(x, amount % 128, 1)


def column(x, v):
    return x[:, 128 * v : 128 * v + 128]


def faces_kernel(
    send_hbm, nb_hbm, feat_hbm, grad_hbm,
    d_ref, c_ref, b_ref, a_ref, nb_ref, feat_ref, grad_ref, send_ref, sems,
):
    copies = [
        pltpu.make_async_copy(send_hbm, send_ref, sems.at[0]),
        pltpu.make_async_copy(nb_hbm, nb_ref, sems.at[17]),
    ]
    for e in range(SLOTS):
        copies.append(pltpu.make_async_copy(feat_hbm.at[e], feat_ref.at[e], sems.at[1 + e]))
        copies.append(pltpu.make_async_copy(grad_hbm.at[e], grad_ref.at[e], sems.at[9 + e]))
    for copy in copies:
        copy.start()
    low = lane(64, 128) < 64
    zero = jnp.zeros((64, 128), BF)
    cell = lax.broadcasted_iota(jnp.int32, (CELLS, 128), 0)
    spot = lane(CELLS, 128)
    same = (cell // 64 == spot // 8 % 8) & (cell % 8 == spot % 8)
    for copy in copies:
        copy.wait()

    def give_low(ref):
        for k in range(CAP):
            e = send_ref[0, k]
            s = jnp.maximum(e, 0)
            v = jnp.where(low, feat_ref[s, :, 0:128], spin(grad_ref[s, :, 0:128], 64))
            ref[k] = jnp.where(e >= 0, v, zero)

    def give_high(ref):
        for k in range(CAP):
            e = send_ref[1, k]
            s = jnp.maximum(e, 0)
            v = jnp.where(low, spin(feat_ref[s, :, 384:512], 64), grad_ref[s, :, 384:512])
            ref[k] = jnp.where(e >= 0, v, zero)

    @pl.when(lax.axis_index("c") == 0)
    def _():
        give_high(a_ref)
        give_low(b_ref)

    @pl.when(lax.axis_index("c") != 0)
    def _():
        give_low(a_ref)
        give_high(b_ref)

    odd = lax.axis_index("ry") % 2
    for ref, t in ((c_ref, 3 - odd), (d_ref, 2 + odd)):
        on = same & (cell // 8 % 8 == 7 * (t - 2))
        pick_feat = jnp.where(on & (spot < 64), 1.0, 0.0).astype(BF)
        pick_grad = jnp.where(on & (spot >= 64), 1.0, 0.0).astype(BF)
        slot = [send_ref[t, k] for k in range(CAP)]
        feats = jnp.concatenate([feat_ref[jnp.maximum(e, 0)] for e in slot], 0)
        grads = jnp.concatenate([grad_ref[jnp.maximum(e, 0)] for e in slot], 0)
        both = jnp.dot(feats, pick_feat, preferred_element_type=F32) + jnp.dot(
            grads, pick_grad, preferred_element_type=F32
        )
        both = both.astype(BF)
        for k in range(CAP):
            ref[k] = jnp.where(slot[k] >= 0, both[64 * k : 64 * k + 64], zero)


def fill_near(live_ref, ref, cubes, xface, tab):
    low = lane(64, 128) < 64
    zero = jnp.zeros((64, 128), BF)
    for e in range(SLOTS):
        alive = e < live_ref[0]
        cols = [jnp.where(alive, ref[e, :, 128 * v : 128 * v + 128], zero) for v in range(4)]
        for v in range(4):
            cubes[e, :, 128 * v : 128 * v + 128] = cols[v]
        xface[0, e] = jnp.where(low, zero, cols[3])
        xface[1, e] = jnp.where(low, cols[0], zero)
    for side in range(2):
        xface[side, NONE] = zero
    tab[NONE] = jnp.zeros((64, 1024), BF)
    source = lax.broadcasted_iota(jnp.int32, (128, 256), 0)
    spot = lane(128, 256)
    place = spot % 128
    from_z = jnp.where(place % 8 == 7, (place + 8) % 128, (place + 120) % 128)
    on_z = (source == from_z) & ((place % 8 == 7) | (place % 8 == 0))
    on_y = source == (place + 64) % 128
    move = jnp.where((on_z & (spot < 128)) | (on_y & (spot >= 128)), 1.0, 0.0).astype(BF)
    for v in range(4):
        many = cubes[0:SLOTS, :, 128 * v : 128 * v + 128].reshape(SLOTS * 64, 128)
        moved = jnp.dot(many, move, preferred_element_type=F32).astype(BF)
        for e in range(SLOTS):
            tab[e, :, 256 * v : 256 * v + 256] = moved[64 * e : 64 * e + 64]


def fill_far(n, got, xface, tab):
    d_ref, c_ref, b_ref, a_ref = got
    low = lane(64, 128) < 64
    zero = jnp.zeros((64, 128), BF)

    def take_x(below, above):
        for k in range(CAP):
            u, v = below[k], above[k]
            xface[0, SLOTS + k] = jnp.where(low, zero, spin(u, 64) if n == 0 else u)
            xface[1, SLOTS + k] = jnp.where(low, v if n == 0 else spin(v, 64), zero)

    pl.when(lax.axis_index("c") == 0)(lambda: take_x(b_ref, a_ref))
    pl.when(lax.axis_index("c") != 0)(lambda: take_x(a_ref, b_ref))
    source = lax.broadcasted_iota(jnp.int32, (128, CELLS), 0)
    cell = lane(128, CELLS)
    layer = cell // 128 * 2 + 1 - cell // 64 % 2
    same = (layer == source // 8 % 8) & (cell % 8 == source % 8) & (source // 64 == n)
    odd = lax.axis_index("ry") % 2
    for got_ref, side in ((c_ref, 1 - odd), (d_ref, odd)):
        put = jnp.where(same & (cell // 8 % 8 == 7 * (1 - side)), 1.0, 0.0).astype(BF)
        packed = got_ref[...].reshape(CAP * 64, 128)
        full = jnp.dot(packed, put, preferred_element_type=F32).astype(BF)

        def keep(offset):
            for k in range(CAP):
                for v in range(4):
                    at = slice(256 * v + 128, 256 * v + 256)
                    tab[SLOTS + offset + k, :, at] = full[
                        64 * k : 64 * k + 64, 128 * v : 128 * v + 128
                    ]

        pl.when(side == 0)(lambda: keep(0))
        pl.when(side != 0)(lambda: keep(CAP))


def fill_windows(g, far, nb_ref, cubes, xface, tab, dst, base):
    def slot(side, step):
        e = nb_ref[g, side]
        near = jnp.minimum(e, SLOTS - 1)
        away = SLOTS + step + ((e - SLOTS) & (CAP - 1)) if far else NONE
        return jnp.where(e < 0, NONE, jnp.where(e < SLOTS, near, away))

    i0, i1 = slot(0, 0), slot(1, 0)
    i2, i3 = slot(2, 0), slot(3, CAP)
    i4, i5 = slot(4, 0), slot(5, 0)
    spots = lane(64, 128)
    plane = spots % 64
    zero = jnp.zeros((64, 128), BF)
    for v in range(5):
        if v < 4:
            at = slice(256 * v, 256 * v + 128)
            up = slice(256 * v + 128, 256 * v + 256)
            mid = cubes[g, :, 128 * v : 128 * v + 128]
            rows = (
                jnp.where(plane // 8 == 7, tab[i2, :, up], mid),
                mid,
                jnp.where(plane // 8 == 0, tab[i3, :, up], mid),
            )
            ends = (tab[i4, :, at], None, tab[i5, :, at])
        else:
            mid = xface[0, i0] + xface[1, i1]
            rows = (
                jnp.where(plane // 8 == 7, zero, mid),
                mid,
                jnp.where(plane // 8 == 0, zero, mid),
            )
            ends = (zero, None, zero)
        for b in range(3):
            for c in range(3):
                x = rows[b]
                if c != 1:
                    z = ends[c]
                    if b != 1 and v < 4:
                        z = jnp.where(plane == CORNER[b, c], zero, z)
                    x = jnp.where(plane % 8 == (7 if c == 0 else 0), z, x)
                shift = 8 * (b - 1) + c - 1
                if shift:
                    x = spin(x, -shift)
                row = 64 * (3 * b + c)
                dst[row : row + 64, base + 128 * v : base + 128 * v + 128] = x


def join_layers(parts, base):
    low = lane(64, 128) < 64

    def col(a, v):
        v = v % 5
        return parts[64 * a : 64 * a + 64, base + 128 * v : base + 128 * v + 128]

    cols = []
    for v in range(4):
        mixed = jnp.where(low, col(0, v) + col(2, v + 1), col(0, v - 1) + col(2, v))
        cols.append((col(1, v) + spin(mixed, 64)).astype(BF))
    return cols


def near_kernel(
    live_ref, nb_ref, feat_ref, grad_ref, acc_ref, shift_ref, rim_ref, cubes, xface, tab, wins
):
    low = lane(64, 128) < 64
    zero = jnp.zeros((64, 128), BF)
    cell = lax.broadcasted_iota(jnp.int32, (CELLS, 128), 0)
    spot = lane(CELLS, 128)
    rim = (cell // 64 == spot // 8 % 8) & (cell % 8 == spot % 8)
    rim = rim & (cell // 8 % 8 == 7 * (spot // 64))
    rim = jnp.where(rim, 1.0, 0.0).astype(BF)
    fill_near(live_ref, feat_ref, cubes, xface, tab)
    for p in range(SLOTS // 2):
        win = wins.at[p % 2]
        for h in range(2):
            g = 2 * p + h
            fill_windows(g, False, nb_ref, cubes, xface, tab, win, WIDE * h)
            alive = g < live_ref[0]
            cols = [
                jnp.where(alive, grad_ref[g, :, 128 * v : 128 * v + 128], zero) for v in range(4)
            ]
            turned = [spin(x, 64) for x in cols]
            for v in range(5):
                at = slice(WIDE * h + 128 * v, WIDE * h + 128 * v + 128)
                here = turned[v] if v < 4 else zero
                left = turned[v - 1] if v > 0 else zero
                right = zero if v == 3 else turned[(v + 1) % 5]
                shift_ref[p, 0:64, at] = jnp.where(low, here, right)
                shift_ref[p, 64:128, at] = cols[v] if v < 4 else zero
                shift_ref[p, 128:192, at] = jnp.where(low, left, here)
            body = shift_ref[p, :, WIDE * h : WIDE * h + CELLS]
            rim_ref[:, 128 * g : 128 * g + 128] = jnp.dot(
                body, rim, preferred_element_type=F32
            ).astype(BF)
        part = lax.dot_general(
            shift_ref[p], win[...], (((1,), (1,)), ((), ())), preferred_element_type=F32
        )
        if p == 0:
            acc_ref[...] = part
        else:
            acc_ref[...] += part


def face_moves():
    source = np.arange(128)[:, None]
    into_x = np.zeros((2, 128, 9 * 128), np.float32)
    into_y = np.zeros((2, 128, 3 * 128), np.float32)
    spot = np.arange(128)[None]
    for side in range(2):
        for b in range(3):
            for c in range(3):
                j, k = spot // 8 % 8 + b - 1, spot % 8 + c - 1
                inside = (j >= 0) & (j < 8) & (k >= 0) & (k < 8) & (spot // 64 == 1 - side)
                col = 128 * (3 * b + c)
                into_x[side, :, col : col + 128] = inside & (source == 8 * j + k)
        for c in range(3):
            k = spot % 8 + c - 1
            inside = (k >= 0) & (k < 8) & (spot // 64 == side)
            into_y[side, :, 128 * c : 128 * c + 128] = inside & (
                source == spot // 8 % 8 * 8 + k
            )
    return jnp.asarray(into_x, BF), jnp.asarray(into_y, BF)


def kernel_grad_kernel(
    nb_ref, near_ref, shift_ref, rim_ref, into_x, into_y, d_ref, c_ref, b_ref, a_ref,
    keep_ref, give_ref, xfar, yfar, ghosts, edges, beyond, acc,
):
    core = lax.axis_index("c")
    odd = lax.axis_index("ry") % 2
    for side in range(2):
        xfar[side, CAP] = jnp.zeros((576, 128), BF)
        yfar[side, CAP] = jnp.zeros((192, 128), BF)
    beyond[192:256] = jnp.zeros((64, 128 * SLOTS), BF)
    for got_ref, side, into, far in (
        (d_ref, odd, into_y, yfar),
        (c_ref, 1 - odd, into_y, yfar),
        (b_ref, core, into_x, xfar),
        (a_ref, 1 - core, into_x, xfar),
    ):
        packed = got_ref[...].reshape(CAP * 64, 128)
        full = jnp.dot(packed, into[side], preferred_element_type=F32).astype(BF)
        for k in range(CAP):
            for n in range(far.shape[2] // 64):
                far[side, k, 64 * n : 64 * n + 64, :] = full[
                    64 * k : 64 * k + 64, 128 * n : 128 * n + 128
                ]
    for g in range(SLOTS):
        p, base = g // 2, WIDE * (g % 2)
        e = [nb_ref[g, side] for side in range(4)]
        i = [jnp.where(x < SLOTS, CAP, (x - SLOTS) & (CAP - 1)) for x in e]
        ghosts[:, 128 * g : 128 * g + 128] = xfar[0, i[0]] + xfar[1, i[1]]
        edges[:, 128 * g : 128 * g + 128] = shift_ref[p, :, base + 512 : base + 640]
        beyond[0:192, 128 * g : 128 * g + 128] = yfar[0, i[2]]
        beyond[256:448, 128 * g : 128 * g + 128] = yfar[1, i[3]]
    rims = lax.dot_general(
        rim_ref[...], beyond[...], (((1,), (1,)), ((), ())), preferred_element_type=F32
    )
    acc[...] = near_ref[...] + lax.dot_general(
        edges[...], ghosts[...], (((1,), (1,)), ((), ())), preferred_element_type=F32
    )
    acc[:, 0:192] += rims[:, 0:192]
    acc[:, 384:576] += rims[:, 256:448]

    def write(first, second):
        for t in range(128):
            ref = first if t < 64 else second
            r, q = t // 5, t % 5
            if t >= 120:
                ref[t % 64] = jnp.zeros((8, 128), F32)
            elif q < 4:
                ref[t % 64] = acc[8 * r : 8 * r + 8, 128 * q : 128 * q + 128]
            else:
                ref[t % 64] = jnp.concatenate(
                    [acc[8 * r : 8 * r + 8, 512:576], jnp.zeros((8, 64), F32)], 1
                )

    pl.when(lax.axis_index("c") == 0)(lambda: write(keep_ref, give_ref))
    pl.when(lax.axis_index("c") != 0)(lambda: write(give_ref, keep_ref))


def conv_kernel(
    n, live_ref, nb_ref, cube_ref, d_ref, c_ref, b_ref, a_ref, w_ref,
    out_hbm, cubes, xface, tab, wins, mat, outs, sems,
):
    zero = jnp.zeros((64, 128), BF)
    eye = lax.broadcasted_iota(jnp.int32, (64, 64), 0) == lane(64, 64)
    eye = jnp.where(eye, 1.0, 0.0).astype(BF)
    for a in range(3):
        if n == 0:
            block = jnp.concatenate([w_ref[9 * a + o] for o in range(9)], axis=1)
        else:
            tall = jnp.concatenate([w_ref[26 - 9 * a - o] for o in range(9)], axis=0)
            block = lax.dot_general(
                eye, tall, (((1,), (1,)), ((), ())), preferred_element_type=F32
            ).astype(BF)
        mat[64 * a : 64 * a + 64] = block
    got = (d_ref, c_ref, b_ref, a_ref)
    fill_near(live_ref, cube_ref, cubes, xface, tab)
    fill_far(n, got, xface, tab)
    copies = []
    for p in range(SLOTS // 2):
        win = wins.at[p % 2]
        for h in range(2):
            fill_windows(2 * p + h, True, nb_ref, cubes, xface, tab, win, WIDE * h)
        parts = jnp.dot(mat[...], win[...], preferred_element_type=F32)
        for h in range(2):
            alive = 2 * p + h < live_ref[0]
            for v, value in enumerate(join_layers(parts, WIDE * h)):
                outs[2 * p + h, :, 128 * v : 128 * v + 128] = jnp.where(alive, value, zero)
        part = pl.ds(2 * p, 2)
        copies.append(pltpu.make_async_copy(outs.at[part], out_hbm.at[part], sems.at[p]))
        copies[-1].start()
    for copy in copies:
        copy.wait()


def spread_kernel(scale, total_ref, out_ref):
    for t in range(120):
        r, q = t // 5, t % 5
        a, co = r // 8, r % 8 * 8
        spot = (t % 64 // 16 * 2 + t // 64) * 16 + t % 16
        tile = total_ref[spot].astype(F32) * scale
        for half in range(2 if q < 4 else 1):
            out_ref[9 * a + 2 * q + half, co : co + 8, :] = tile[:, 64 * half : 64 * half + 64]


def swaps(count, first):
    pairs = [(i, (i + 1) % count) for i in range(first, count + first, 2)]
    return pairs + [(j, i) for i, j in pairs]


def body(features, grad_out, weights, live_count, neighbor, send_list):
    params = pltpu.CompilerParams(vmem_limit_bytes=50 * 1024 * 1024)
    n_rows = lax.axis_size("z") * lax.axis_size("c")
    n_cols = lax.axis_size("ry")
    face = jax.ShapeDtypeStruct((CAP, 64, 128), BF)
    cells = jax.ShapeDtypeStruct((SLOTS, 64, CELLS), BF)
    give_d, give_c, give_b, give_a, neighbor, features, grad_out = pl.pallas_call(
        faces_kernel,
        out_shape=(face,) * 4 + (jax.ShapeDtypeStruct((SLOTS, 6), jnp.int32), cells, cells),
        in_specs=[HBM_SPEC] * 4,
        out_specs=(VMEM_SPEC,) * 7,
        scratch_shapes=[pltpu.SMEM((4, CAP), jnp.int32), pltpu.SemaphoreType.DMA((18,))],
        compiler_params=pltpu.CompilerParams(vmem_limit_bytes=48 * 1024 * 1024),
        name="faces",
    )(*(pltpu.with_memory_space_constraint(x, pltpu.HBM) for x in (send_list, neighbor, features, grad_out)))
    got_d = lax.ppermute(give_d, "ry", swaps(n_cols, 1))
    got_c = lax.ppermute(give_c, "ry", swaps(n_cols, 0))
    got_b = lax.ppermute(give_b, ("z", "c"), swaps(n_rows, 1))
    got_a = lax.ppermute(give_a, ("z", "c"), swaps(n_rows, 0))
    got = (got_d, got_c, got_b, got_a)
    tables = [
        pltpu.VMEM((SLOTS + 1, 64, CELLS), BF),
        pltpu.VMEM((2, NONE + 1, 64, 128), BF),
        pltpu.VMEM((NONE + 1, 64, 1024), BF),
    ]
    half = jax.ShapeDtypeStruct((64, 8, 128), F32)
    flops = 2 * 192 * 576 * SLOTS * WIDE
    cost = pl.CostEstimate(flops=2 * flops, bytes_accessed=8 << 20, transcendentals=0)
    small = pltpu.CompilerParams(vmem_limit_bytes=24 * 1024 * 1024)
    near, shifted, rims = pl.pallas_call(
        near_kernel,
        out_shape=(
            jax.ShapeDtypeStruct((192, 576), F32),
            jax.ShapeDtypeStruct((SLOTS // 2, 192, 2 * WIDE), BF),
            jax.ShapeDtypeStruct((192, 128 * SLOTS), BF),
        ),
        in_specs=[SMEM_SPEC] * 2 + [VMEM_SPEC] * 2,
        out_specs=(VMEM_SPEC,) * 3,
        scratch_shapes=tables + [pltpu.VMEM((2, 576, 2 * WIDE), BF)],
        compiler_params=small,
        cost_estimate=cost,
        name="near_pairs",
    )(live_count, neighbor, features, grad_out)
    keep, give = pl.pallas_call(
        kernel_grad_kernel,
        out_shape=(half, half),
        in_specs=[SMEM_SPEC] + [VMEM_SPEC] * 9,
        out_specs=(VMEM_SPEC, VMEM_SPEC),
        scratch_shapes=[
            pltpu.VMEM((2, CAP + 1, 576, 128), BF),
            pltpu.VMEM((2, CAP + 1, 192, 128), BF),
            pltpu.VMEM((576, 128 * SLOTS), BF),
            pltpu.VMEM((192, 128 * SLOTS), BF),
            pltpu.VMEM((448, 128 * SLOTS), BF),
            pltpu.VMEM((192, 576), F32),
        ],
        compiler_params=small,
        cost_estimate=cost,
        name="kernel_grad",
    )(neighbor, near, shifted, rims, *face_moves(), *got)

    def convolve(n, cubes, w, name):
        return pl.pallas_call(
            lambda *refs: conv_kernel(n, *refs),
            out_shape=jax.ShapeDtypeStruct((SLOTS, 64, CELLS), BF),
            in_specs=[SMEM_SPEC] * 2 + [VMEM_SPEC] * 6,
            out_specs=HBM_SPEC,
            scratch_shapes=tables
            + [
                pltpu.VMEM((2, 576, 2 * WIDE), BF),
                pltpu.VMEM((192, 576), BF),
                pltpu.VMEM((SLOTS, 64, CELLS), BF),
                pltpu.SemaphoreType.DMA((SLOTS // 2,)),
            ],
            compiler_params=small,
            cost_estimate=cost,
            name=name,
        )(live_count, neighbor, cubes, *got, w)

    mine = keep + lax.ppermute(give, "c", [(0, 1), (1, 0)])
    output = convolve(0, features, weights, "forward")
    grad_features = convolve(1, grad_out, weights, "input_grad")
    terms = lax.all_to_all(mine, ("z", "ry"), 0, 0, tiled=True)
    total = jnp.sum(terms, axis=0, keepdims=True).astype(BF)
    total, output = lax.optimization_barrier((total, output))
    spread = jnp.broadcast_to(total, (n_rows * n_cols, 8, 128))
    totals = lax.all_to_all(spread, ("z", "c", "ry"), 0, 0, tiled=True)
    scale = (512.0 * SLOTS * n_rows * n_cols) ** (-0.5)
    grad_weights = pl.pallas_call(
        lambda *refs: spread_kernel(scale, *refs),
        out_shape=jax.ShapeDtypeStruct((27, 64, 64), F32),
        in_specs=[VMEM_SPEC],
        out_specs=VMEM_SPEC,
        compiler_params=params,
        name="spread",
    )(totals)
    return output, grad_features, grad_weights


def solution(mesh):
    split = Mesh(mesh.devices.reshape(4, 2, 16), ("z", "c", "ry"))
    rows = P(("z", "c", "ry"))
    return jax.shard_map(
        body,
        mesh=split,
        in_specs=(rows, rows, P(), rows, rows, rows),
        out_specs=(rows, rows, P()),
        check_vma=False,
    )
```

```python
import jax
import jax.numpy as jnp
import numpy as np
from jax import lax
from jax.experimental import pallas as pl
from jax.experimental.pallas import tpu as pltpu
from jax.sharding import Mesh
from jax.sharding import PartitionSpec as P

BF = jnp.bfloat16
F32 = jnp.float32
VMEM_SPEC = pl.BlockSpec(memory_space=pltpu.VMEM)
SMEM_SPEC = pl.BlockSpec(memory_space=pltpu.SMEM)
SLOTS = 8
CAP = 4
NONE = SLOTS + 2 * CAP
CELLS = 512
WIDE = 640
CORNER = {(0, 0): 55, (2, 0): 63, (0, 2): 0, (2, 2): 8}
HBM_SPEC = pl.BlockSpec(memory_space=pltpu.HBM)


def lane(rows, cols):
    return lax.broadcasted_iota(jnp.int32, (rows, cols), 1)


def spin(x, amount):
    return pltpu.roll(x, amount % 128, 1)


def column(x, v):
    return x[:, 128 * v : 128 * v + 128]


def faces_kernel(
    send_hbm, nb_hbm, feat_hbm, grad_hbm,
    d_ref, c_ref, b_ref, a_ref, nb_ref, feat_ref, grad_ref, send_ref, sems,
):
    copies = [
        pltpu.make_async_copy(send_hbm, send_ref, sems.at[0]),
        pltpu.make_async_copy(nb_hbm, nb_ref, sems.at[17]),
    ]
    for e in range(SLOTS):
        copies.append(pltpu.make_async_copy(feat_hbm.at[e], feat_ref.at[e], sems.at[1 + e]))
        copies.append(pltpu.make_async_copy(grad_hbm.at[e], grad_ref.at[e], sems.at[9 + e]))
    for copy in copies:
        copy.start()
    low = lane(64, 128) < 64
    zero = jnp.zeros((64, 128), BF)
    cell = lax.broadcasted_iota(jnp.int32, (CELLS, 128), 0)
    spot = lane(CELLS, 128)
    same = (cell // 64 == spot // 8 % 8) & (cell % 8 == spot % 8)
    for copy in copies:
        copy.wait()

    def give_low(ref):
        for k in range(CAP):
            e = send_ref[0, k]
            s = jnp.maximum(e, 0)
            v = jnp.where(low, feat_ref[s, :, 0:128], spin(grad_ref[s, :, 0:128], 64))
            ref[k] = jnp.where(e >= 0, v, zero)

    def give_high(ref):
        for k in range(CAP):
            e = send_ref[1, k]
            s = jnp.maximum(e, 0)
            v = jnp.where(low, spin(feat_ref[s, :, 384:512], 64), grad_ref[s, :, 384:512])
            ref[k] = jnp.where(e >= 0, v, zero)

    @pl.when(lax.axis_index("c") == 0)
    def _():
        give_high(a_ref)
        give_low(b_ref)

    @pl.when(lax.axis_index("c") != 0)
    def _():
        give_low(a_ref)
        give_high(b_ref)

    odd = lax.axis_index("ry") % 2
    for ref, t in ((c_ref, 3 - odd), (d_ref, 2 + odd)):
        on = same & (cell // 8 % 8 == 7 * (t - 2))
        pick_feat = jnp.where(on & (spot < 64), 1.0, 0.0).astype(BF)
        pick_grad = jnp.where(on & (spot >= 64), 1.0, 0.0).astype(BF)
        slot = [send_ref[t, k] for k in range(CAP)]
        feats = jnp.concatenate([feat_ref[jnp.maximum(e, 0)] for e in slot], 0)
        grads = jnp.concatenate([grad_ref[jnp.maximum(e, 0)] for e in slot], 0)
        both = jnp.dot(feats, pick_feat, preferred_element_type=F32) + jnp.dot(
            grads, pick_grad, preferred_element_type=F32
        )
        both = both.astype(BF)
        for k in range(CAP):
            ref[k] = jnp.where(slot[k] >= 0, both[64 * k : 64 * k + 64], zero)


def fill_near(live_ref, ref, cubes, xface, tab):
    low = lane(64, 128) < 64
    zero = jnp.zeros((64, 128), BF)
    for e in range(SLOTS):
        alive = e < live_ref[0]
        cols = [jnp.where(alive, ref[e, :, 128 * v : 128 * v + 128], zero) for v in range(4)]
        for v in range(4):
            cubes[e, :, 128 * v : 128 * v + 128] = cols[v]
        xface[0, e] = jnp.where(low, zero, cols[3])
        xface[1, e] = jnp.where(low, cols[0], zero)
    for side in range(2):
        xface[side, NONE] = zero
    tab[NONE] = jnp.zeros((64, 1024), BF)
    source = lax.broadcasted_iota(jnp.int32, (128, 256), 0)
    spot = lane(128, 256)
    place = spot % 128
    from_z = jnp.where(place % 8 == 7, (place + 8) % 128, (place + 120) % 128)
    on_z = (source == from_z) & ((place % 8 == 7) | (place % 8 == 0))
    on_y = source == (place + 64) % 128
    move = jnp.where((on_z & (spot < 128)) | (on_y & (spot >= 128)), 1.0, 0.0).astype(BF)
    for v in range(4):
        many = cubes[0:SLOTS, :, 128 * v : 128 * v + 128].reshape(SLOTS * 64, 128)
        moved = jnp.dot(many, move, preferred_element_type=F32).astype(BF)
        for e in range(SLOTS):
            tab[e, :, 256 * v : 256 * v + 256] = moved[64 * e : 64 * e + 64]


def fill_far(n, got, xface, tab):
    d_ref, c_ref, b_ref, a_ref = got
    low = lane(64, 128) < 64
    zero = jnp.zeros((64, 128), BF)

    def take_x(below, above):
        for k in range(CAP):
            u, v = below[k], above[k]
            xface[0, SLOTS + k] = jnp.where(low, zero, spin(u, 64) if n == 0 else u)
            xface[1, SLOTS + k] = jnp.where(low, v if n == 0 else spin(v, 64), zero)

    pl.when(lax.axis_index("c") == 0)(lambda: take_x(b_ref, a_ref))
    pl.when(lax.axis_index("c") != 0)(lambda: take_x(a_ref, b_ref))
    source = lax.broadcasted_iota(jnp.int32, (128, CELLS), 0)
    cell = lane(128, CELLS)
    layer = cell // 128 * 2 + 1 - cell // 64 % 2
    same = (layer == source // 8 % 8) & (cell % 8 == source % 8) & (source // 64 == n)
    odd = lax.axis_index("ry") % 2
    for got_ref, side in ((c_ref, 1 - odd), (d_ref, odd)):
        put = jnp.where(same & (cell // 8 % 8 == 7 * (1 - side)), 1.0, 0.0).astype(BF)
        packed = got_ref[...].reshape(CAP * 64, 128)
        full = jnp.dot(packed, put, preferred_element_type=F32).astype(BF)

        def keep(offset):
            for k in range(CAP):
                for v in range(4):
                    at = slice(256 * v + 128, 256 * v + 256)
                    tab[SLOTS + offset + k, :, at] = full[
                        64 * k : 64 * k + 64, 128 * v : 128 * v + 128
                    ]

        pl.when(side == 0)(lambda: keep(0))
        pl.when(side != 0)(lambda: keep(CAP))


def fill_windows(g, far, nb_ref, cubes, xface, tab, dst, base):
    def slot(side, step):
        e = nb_ref[g, side]
        near = jnp.minimum(e, SLOTS - 1)
        away = SLOTS + step + ((e - SLOTS) & (CAP - 1)) if far else NONE
        return jnp.where(e < 0, NONE, jnp.where(e < SLOTS, near, away))

    i0, i1 = slot(0, 0), slot(1, 0)
    i2, i3 = slot(2, 0), slot(3, CAP)
    i4, i5 = slot(4, 0), slot(5, 0)
    spots = lane(64, 128)
    plane = spots % 64
    zero = jnp.zeros((64, 128), BF)
    for v in range(5):
        if v < 4:
            at = slice(256 * v, 256 * v + 128)
            up = slice(256 * v + 128, 256 * v + 256)
            mid = cubes[g, :, 128 * v : 128 * v + 128]
            rows = (
                jnp.where(plane // 8 == 7, tab[i2, :, up], mid),
                mid,
                jnp.where(plane // 8 == 0, tab[i3, :, up], mid),
            )
            ends = (tab[i4, :, at], None, tab[i5, :, at])
        else:
            mid = xface[0, i0] + xface[1, i1]
            rows = (
                jnp.where(plane // 8 == 7, zero, mid),
                mid,
                jnp.where(plane // 8 == 0, zero, mid),
            )
            ends = (zero, None, zero)
        for b in range(3):
            for c in range(3):
                x = rows[b]
                if c != 1:
                    z = ends[c]
                    if b != 1 and v < 4:
                        z = jnp.where(plane == CORNER[b, c], zero, z)
                    x = jnp.where(plane % 8 == (7 if c == 0 else 0), z, x)
                shift = 8 * (b - 1) + c - 1
                if shift:
                    x = spin(x, -shift)
                row = 64 * (3 * b + c)
                dst[row : row + 64, base + 128 * v : base + 128 * v + 128] = x


def join_layers(parts, base):
    low = lane(64, 128) < 64

    def col(a, v):
        v = v % 5
        return parts[64 * a : 64 * a + 64, base + 128 * v : base + 128 * v + 128]

    cols = []
    for v in range(4):
        mixed = jnp.where(low, col(0, v) + col(2, v + 1), col(0, v - 1) + col(2, v))
        cols.append((col(1, v) + spin(mixed, 64)).astype(BF))
    return cols


def near_kernel(
    live_ref, nb_ref, feat_ref, grad_ref, acc_ref, shift_ref, rim_ref, cubes, xface, tab, wins
):
    low = lane(64, 128) < 64
    zero = jnp.zeros((64, 128), BF)
    cell = lax.broadcasted_iota(jnp.int32, (CELLS, 128), 0)
    spot = lane(CELLS, 128)
    rim = (cell // 64 == spot // 8 % 8) & (cell % 8 == spot % 8)
    rim = rim & (cell // 8 % 8 == 7 * (spot // 64))
    rim = jnp.where(rim, 1.0, 0.0).astype(BF)
    fill_near(live_ref, feat_ref, cubes, xface, tab)
    for p in range(SLOTS // 2):
        win = wins.at[p % 2]
        for h in range(2):
            g = 2 * p + h
            fill_windows(g, False, nb_ref, cubes, xface, tab, win, WIDE * h)
            alive = g < live_ref[0]
            cols = [
                jnp.where(alive, grad_ref[g, :, 128 * v : 128 * v + 128], zero) for v in range(4)
            ]
            turned = [spin(x, 64) for x in cols]
            for v in range(5):
                at = slice(WIDE * h + 128 * v, WIDE * h + 128 * v + 128)
                here = turned[v] if v < 4 else zero
                left = turned[v - 1] if v > 0 else zero
                right = zero if v == 3 else turned[(v + 1) % 5]
                shift_ref[p, 0:64, at] = jnp.where(low, here, right)
                shift_ref[p, 64:128, at] = cols[v] if v < 4 else zero
                shift_ref[p, 128:192, at] = jnp.where(low, left, here)
            body = shift_ref[p, :, WIDE * h : WIDE * h + CELLS]
            rim_ref[:, 128 * g : 128 * g + 128] = jnp.dot(
                body, rim, preferred_element_type=F32
            ).astype(BF)
        part = lax.dot_general(
            shift_ref[p], win[...], (((1,), (1,)), ((), ())), preferred_element_type=F32
        )
        if p == 0:
            acc_ref[...] = part
        else:
            acc_ref[...] += part


def face_moves():
    source = np.arange(128)[:, None]
    into_x = np.zeros((2, 128, 9 * 128), np.float32)
    into_y = np.zeros((2, 128, 3 * 128), np.float32)
    spot = np.arange(128)[None]
    for side in range(2):
        for b in range(3):
            for c in range(3):
                j, k = spot // 8 % 8 + b - 1, spot % 8 + c - 1
                inside = (j >= 0) & (j < 8) & (k >= 0) & (k < 8) & (spot // 64 == 1 - side)
                col = 128 * (3 * b + c)
                into_x[side, :, col : col + 128] = inside & (source == 8 * j + k)
        for c in range(3):
            k = spot % 8 + c - 1
            inside = (k >= 0) & (k < 8) & (spot // 64 == side)
            into_y[side, :, 128 * c : 128 * c + 128] = inside & (
                source == spot // 8 % 8 * 8 + k
            )
    return jnp.asarray(into_x, BF), jnp.asarray(into_y, BF)


def kernel_grad_kernel(
    nb_ref, near_ref, shift_ref, rim_ref, into_x, into_y, d_ref, b_ref, c_ref, a_ref,
    keep_ref, give_ref, xfar, yfar, ghosts, edges, beyond, acc,
):
    core = lax.axis_index("c")
    odd = lax.axis_index("ry") % 2
    for side in range(2):
        xfar[side, CAP] = jnp.zeros((576, 128), BF)
        yfar[side, CAP] = jnp.zeros((192, 128), BF)
    beyond[192:256] = jnp.zeros((64, 128 * SLOTS), BF)
    for got_ref, side, into, far in (
        (d_ref, odd, into_y, yfar),
        (c_ref, 1 - odd, into_y, yfar),
        (b_ref, core, into_x, xfar),
        (a_ref, 1 - core, into_x, xfar),
    ):
        packed = got_ref[...].reshape(CAP * 64, 128)
        full = jnp.dot(packed, into[side], preferred_element_type=F32).astype(BF)
        for k in range(CAP):
            for n in range(far.shape[2] // 64):
                far[side, k, 64 * n : 64 * n + 64, :] = full[
                    64 * k : 64 * k + 64, 128 * n : 128 * n + 128
                ]
    for g in range(SLOTS):
        p, base = g // 2, WIDE * (g % 2)
        e = [nb_ref[g, side] for side in range(4)]
        i = [jnp.where(x < SLOTS, CAP, (x - SLOTS) & (CAP - 1)) for x in e]
        ghosts[:, 128 * g : 128 * g + 128] = xfar[0, i[0]] + xfar[1, i[1]]
        edges[:, 128 * g : 128 * g + 128] = shift_ref[p, :, base + 512 : base + 640]
        beyond[0:192, 128 * g : 128 * g + 128] = yfar[0, i[2]]
        beyond[256:448, 128 * g : 128 * g + 128] = yfar[1, i[3]]
    rims = lax.dot_general(
        rim_ref[...], beyond[...], (((1,), (1,)), ((), ())), preferred_element_type=F32
    )
    acc[...] = near_ref[...] + lax.dot_general(
        edges[...], ghosts[...], (((1,), (1,)), ((), ())), preferred_element_type=F32
    )
    acc[:, 0:192] += rims[:, 0:192]
    acc[:, 384:576] += rims[:, 256:448]

    def write(first, second):
        for t in range(128):
            ref = first if t < 64 else second
            r, q = t // 5, t % 5
            if t >= 120:
                ref[t % 64] = jnp.zeros((8, 128), F32)
            elif q < 4:
                ref[t % 64] = acc[8 * r : 8 * r + 8, 128 * q : 128 * q + 128]
            else:
                ref[t % 64] = jnp.concatenate(
                    [acc[8 * r : 8 * r + 8, 512:576], jnp.zeros((8, 64), F32)], 1
                )

    pl.when(lax.axis_index("c") == 0)(lambda: write(keep_ref, give_ref))
    pl.when(lax.axis_index("c") != 0)(lambda: write(give_ref, keep_ref))


def conv_kernel(
    n, live_ref, nb_ref, cube_ref, d_ref, b_ref, c_ref, a_ref, w_ref,
    out_hbm, cubes, xface, tab, wins, mat, outs, sems,
):
    zero = jnp.zeros((64, 128), BF)
    eye = lax.broadcasted_iota(jnp.int32, (64, 64), 0) == lane(64, 64)
    eye = jnp.where(eye, 1.0, 0.0).astype(BF)
    for a in range(3):
        if n == 0:
            block = jnp.concatenate([w_ref[9 * a + o] for o in range(9)], axis=1)
        else:
            tall = jnp.concatenate([w_ref[26 - 9 * a - o] for o in range(9)], axis=0)
            block = lax.dot_general(
                eye, tall, (((1,), (1,)), ((), ())), preferred_element_type=F32
            ).astype(BF)
        mat[64 * a : 64 * a + 64] = block
    got = (d_ref, c_ref, b_ref, a_ref)
    fill_near(live_ref, cube_ref, cubes, xface, tab)
    fill_far(n, got, xface, tab)
    copies = []
    for p in range(SLOTS // 2):
        win = wins.at[p % 2]
        for h in range(2):
            fill_windows(2 * p + h, True, nb_ref, cubes, xface, tab, win, WIDE * h)
        parts = jnp.dot(mat[...], win[...], preferred_element_type=F32)
        for h in range(2):
            alive = 2 * p + h < live_ref[0]
            for v, value in enumerate(join_layers(parts, WIDE * h)):
                outs[2 * p + h, :, 128 * v : 128 * v + 128] = jnp.where(alive, value, zero)
        part = pl.ds(2 * p, 2)
        copies.append(pltpu.make_async_copy(outs.at[part], out_hbm.at[part], sems.at[p]))
        copies[-1].start()
    for copy in copies:
        copy.wait()


def spread_kernel(scale, total_ref, out_ref):
    for t in range(120):
        r, q = t // 5, t % 5
        a, co = r // 8, r % 8 * 8
        spot = (t % 64 // 16 * 2 + t // 64) * 16 + t % 16
        tile = total_ref[spot].astype(F32) * scale
        for half in range(2 if q < 4 else 1):
            out_ref[9 * a + 2 * q + half, co : co + 8, :] = tile[:, 64 * half : 64 * half + 64]


def swaps(count, first):
    pairs = [(i, (i + 1) % count) for i in range(first, count + first, 2)]
    return pairs + [(j, i) for i, j in pairs]


def body(features, grad_out, weights, live_count, neighbor, send_list):
    params = pltpu.CompilerParams(vmem_limit_bytes=50 * 1024 * 1024)
    n_rows = lax.axis_size("z") * lax.axis_size("c")
    n_cols = lax.axis_size("ry")
    face = jax.ShapeDtypeStruct((CAP, 64, 128), BF)
    cells = jax.ShapeDtypeStruct((SLOTS, 64, CELLS), BF)
    give_d, give_c, give_b, give_a, neighbor, features, grad_out = pl.pallas_call(
        faces_kernel,
        out_shape=(face,) * 4 + (jax.ShapeDtypeStruct((SLOTS, 6), jnp.int32), cells, cells),
        in_specs=[HBM_SPEC] * 4,
        out_specs=(VMEM_SPEC,) * 7,
        scratch_shapes=[pltpu.SMEM((4, CAP), jnp.int32), pltpu.SemaphoreType.DMA((18,))],
        compiler_params=pltpu.CompilerParams(vmem_limit_bytes=48 * 1024 * 1024),
        name="faces",
    )(*(pltpu.with_memory_space_constraint(x, pltpu.HBM) for x in (send_list, neighbor, features, grad_out)))
    got_d = lax.ppermute(give_d, "ry", swaps(n_cols, 1))
    got_c = lax.ppermute(give_c, "ry", swaps(n_cols, 0))
    got_b = lax.ppermute(give_b, ("z", "c"), swaps(n_rows, 1))
    got_a = lax.ppermute(give_a, ("z", "c"), swaps(n_rows, 0))
    got = (got_d, got_b, got_c, got_a)
    tables = [
        pltpu.VMEM((SLOTS + 1, 64, CELLS), BF),
        pltpu.VMEM((2, NONE + 1, 64, 128), BF),
        pltpu.VMEM((NONE + 1, 64, 1024), BF),
    ]
    half = jax.ShapeDtypeStruct((64, 8, 128), F32)
    flops = 2 * 192 * 576 * SLOTS * WIDE
    cost = pl.CostEstimate(flops=2 * flops, bytes_accessed=8 << 20, transcendentals=0)
    small = pltpu.CompilerParams(vmem_limit_bytes=24 * 1024 * 1024)
    near, shifted, rims = pl.pallas_call(
        near_kernel,
        out_shape=(
            jax.ShapeDtypeStruct((192, 576), F32),
            jax.ShapeDtypeStruct((SLOTS // 2, 192, 2 * WIDE), BF),
            jax.ShapeDtypeStruct((192, 128 * SLOTS), BF),
        ),
        in_specs=[SMEM_SPEC] * 2 + [VMEM_SPEC] * 2,
        out_specs=(VMEM_SPEC,) * 3,
        scratch_shapes=tables + [pltpu.VMEM((2, 576, 2 * WIDE), BF)],
        compiler_params=small,
        cost_estimate=cost,
        name="near_pairs",
    )(live_count, neighbor, features, grad_out)
    keep, give = pl.pallas_call(
        kernel_grad_kernel,
        out_shape=(half, half),
        in_specs=[SMEM_SPEC] + [VMEM_SPEC] * 9,
        out_specs=(VMEM_SPEC, VMEM_SPEC),
        scratch_shapes=[
            pltpu.VMEM((2, CAP + 1, 576, 128), BF),
            pltpu.VMEM((2, CAP + 1, 192, 128), BF),
            pltpu.VMEM((576, 128 * SLOTS), BF),
            pltpu.VMEM((192, 128 * SLOTS), BF),
            pltpu.VMEM((448, 128 * SLOTS), BF),
            pltpu.VMEM((192, 576), F32),
        ],
        compiler_params=small,
        cost_estimate=cost,
        name="kernel_grad",
    )(neighbor, near, shifted, rims, *face_moves(), *got)

    def convolve(n, cubes, w, name):
        return pl.pallas_call(
            lambda *refs: conv_kernel(n, *refs),
            out_shape=jax.ShapeDtypeStruct((SLOTS, 64, CELLS), BF),
            in_specs=[SMEM_SPEC] * 2 + [VMEM_SPEC] * 6,
            out_specs=HBM_SPEC,
            scratch_shapes=tables
            + [
                pltpu.VMEM((2, 576, 2 * WIDE), BF),
                pltpu.VMEM((192, 576), BF),
                pltpu.VMEM((SLOTS, 64, CELLS), BF),
                pltpu.SemaphoreType.DMA((SLOTS // 2,)),
            ],
            compiler_params=small,
            cost_estimate=cost,
            name=name,
        )(live_count, neighbor, cubes, *got, w)

    mine = keep + lax.ppermute(give, "c", [(0, 1), (1, 0)])
    output = convolve(0, features, weights, "forward")
    grad_features = convolve(1, grad_out, weights, "input_grad")
    terms = lax.all_to_all(mine, ("z", "ry"), 0, 0, tiled=True)
    total = jnp.sum(terms, axis=0, keepdims=True).astype(BF)
    total, output = lax.optimization_barrier((total, output))
    spread = jnp.broadcast_to(total, (n_rows * n_cols, 8, 128))
    totals = lax.all_to_all(spread, ("z", "c", "ry"), 0, 0, tiled=True)
    scale = (512.0 * SLOTS * n_rows * n_cols) ** (-0.5)
    grad_weights = pl.pallas_call(
        lambda *refs: spread_kernel(scale, *refs),
        out_shape=jax.ShapeDtypeStruct((27, 64, 64), F32),
        in_specs=[VMEM_SPEC],
        out_specs=VMEM_SPEC,
        compiler_params=params,
        name="spread",
    )(totals)
    return output, grad_features, grad_weights


def solution(mesh):
    split = Mesh(mesh.devices.reshape(4, 2, 16), ("z", "c", "ry"))
    rows = P(("z", "c", "ry"))
    return jax.shard_map(
        body,
        mesh=split,
        in_specs=(rows, rows, P(), rows, rows, rows),
        out_specs=(rows, rows, P()),
        check_vma=False,
    )
```
